256 devices in a mesh: grp: 16 (over y_lo, z), blk: 8 (over x, core), tp: 2 (over y_hi).
Axes of the slice: x: 4, y: 4 (y_hi: 2, y_lo: 2; y = y_hi * 2 + y_lo), z: 8, core: 2. Of those that a mesh axis runs over, the one named last changes fastest.
Arguments:
- queries: bfloat16 [2048, 4096], P('grp', ('blk', 'tp')), may hold values from -110 to 110
- keys: bfloat16 [2048, 4096], P('grp', ('blk', 'tp')), may hold values from -5 to 5
- values: bfloat16 [2048, 4096], P('grp', ('blk', 'tp')), may hold values from -6 to 6
- cross_queries: bfloat16 [2048, 4096], P('grp', ('blk', 'tp')), may hold values from -110 to 110
- history_keys: bfloat16 [3072, 4096], P('grp', ('blk', 'tp')), may hold values from -5 to 5
- history_values: bfloat16 [3072, 4096], P('grp', ('blk', 'tp')), may hold values from -6 to 6
- frame_ids: int32 [2048], replicated, may hold values from 0 to 31, never falling along the last dimension, each value on 1 to 128 neighbouring positions
- masked: int32 [2048], replicated, may hold values 0 or 1
- out_weight: bfloat16 [4096, 5120], P(('blk', 'tp')), may hold values from -0.09375 to 0.09375
- cotangent: bfloat16 [2048, 5120], P('grp', ('blk', 'tp')), may hold values from -6 to 6
Outputs:
- layer_out: bfloat16 [2048, 5120], P('grp', ('blk', 'tp'))
- query_grad: bfloat16 [2048, 4096], P('grp', ('blk', 'tp'))
- key_grad: bfloat16 [2048, 4096], P('grp', ('blk', 'tp'))
- value_grad: bfloat16 [2048, 4096], P('grp', ('blk', 'tp'))
- cross_query_grad: bfloat16 [2048, 4096], P('grp', ('blk', 'tp'))
- history_key_grad: bfloat16 [3072, 4096], P('grp', ('blk', 'tp'))
- history_value_grad: bfloat16 [3072, 4096], P('grp', ('blk', 'tp'))
- weight_grad: float32 [4096, 5120], P(('blk', 'tp'), 'grp')
The draws below stay inside these ranges and needn't reach their ends.
Inputs may be any that keep to these rules, and one draw needn't show every extreme that they name: `frame_ids`: frame numbers never fall along the tokens; a frame holds 1 to 128 tokens.
All inputs are finite; a program needn't handle non-finite values.
Results may differ from the reference program's by a relative error of at most 0.017.
Values may be sent and summed in bfloat16 or wider, within the bound.
A program may use at most 128 MiB of HBM per device.

```python
import math
import jax
import jax.numpy as jnp
import numpy as np
from jax import lax

D = 5120
HEADS = 32
HD = 128
TOKENS = 2048
HISTORY = 3072
FRAMES = 32
FRAME_MOST = 128


def self_pair(key):
    base = jax.random.fold_in(key, 101)
    key_query, key_key = jax.random.split(base, 2)
    width = HEADS * HD
    keys_all = jnp.clip(jax.random.normal(key_key, (TOKENS, width), jnp.float32), -4.5, 4.5)
    queries_all = jnp.clip(jax.random.normal(key_query, (TOKENS, width), jnp.float32), -4.5, 4.5)
    return (queries_all, keys_all)


def cross_pair(key):
    base = jax.random.fold_in(key, 202)
    key_query, key_key = jax.random.split(base, 2)
    width = HEADS * HD
    memory = jnp.clip(jax.random.normal(key_key, (HISTORY, width), jnp.float32), -4.5, 4.5)
    asking = jnp.clip(jax.random.normal(key_query, (TOKENS, width), jnp.float32), -4.5, 4.5)
    return (asking, memory)


def draw_queries(key, part):
    return self_pair(key)[0].astype(jnp.bfloat16)


def draw_keys(key, part):
    return self_pair(key)[1].astype(jnp.bfloat16)


def draw_cross_queries(key, part):
    return cross_pair(key)[0].astype(jnp.bfloat16)


def draw_history_keys(key, part):
    return cross_pair(key)[1].astype(jnp.bfloat16)


def place_ends(drawn, rng, smallest, high):
    index_at = [jax.random.randint(jax.random.fold_in(rng, axis), (), 0, length) for axis, length in enumerate(drawn.shape)]
    longest = drawn.shape.index(max(drawn.shape))
    neighbour = index_at[:longest] + [(index_at[longest] + 1) % drawn.shape[longest]] + index_at[longest + 1:]
    return drawn.at[tuple(index_at)].set(smallest).at[tuple(neighbour)].set(high)


def strengthened(array, rng, source, target, blocks, factor):
    def block_of(axis_at):
        return (jnp.arange(array.shape[axis_at]) // (array.shape[axis_at] // blocks)).reshape((-1,) + (1,) * (array.ndim - 1 - axis_at))

    first = jax.random.permutation(rng, blocks)[block_of(target)]
    other_side = (block_of(target) + blocks // 2) % blocks
    return jnp.where((block_of(source) == first) | (block_of(source) == other_side), factor * array, array)


def level_of(key, shape, cuts, smallest, high):
    level, own = 1.0, jax.random.fold_in(key, 6)
    for dim, parts in cuts:
        heights = jnp.exp(jax.random.uniform(jax.random.fold_in(own, dim), (parts,), jnp.float32, smallest / len(cuts), high / len(cuts)))
        level = level * jnp.repeat(heights, shape[dim] // parts).reshape([-1 if axis == dim else 1 for axis in range(len(shape))])
    return level


def split_up(number_of, total, limit, lean):
    weights = [(1 << 20) // math.isqrt(grade ** lean) + 1 for grade in range(2, number_of + 1)]
    rest, counts = total - limit - (number_of - 1), [1] * (number_of - 1)
    while rest > 0:
        candidates = [i for i in range(number_of - 1) if counts[i] < limit]
        mass, remaining = sum([weights[i] for i in candidates]), rest
        for i in candidates:
            more = min(limit - counts[i], max(1, remaining * weights[i] // mass), rest)
            counts[i] = counts[i] + more
            rest = rest - more
    return np.array([limit] + counts)


def uneven_parts(rng, number_of, total, most, skew):
    if number_of == 2:
        one = jax.random.randint(rng, (), max(1, total - most), min(most, total - 1) + 1)
        return jnp.stack([one, total - one])
    sizes = jnp.asarray(split_up(number_of, total, most, skew), jnp.int32)
    couples = (number_of - 1) // 2
    donor, taker = sizes[1:1 + 2 * couples:2], sizes[2:2 + 2 * couples:2]
    room = jnp.minimum(donor - 1, most - taker)
    passed = jax.random.randint(jax.random.fold_in(rng, 1), (couples,), 0, 1 << 20) % (room + 1)
    sizes = sizes.at[1:1 + 2 * couples:2].set(donor - passed).at[2:2 + 2 * couples:2].set(taker + passed)
    return sizes[jax.random.permutation(jax.random.fold_in(rng, 2), number_of)]


def normal_values(rng, shape, deviation, most, pieces=(), kind=jnp.bfloat16):
    array = deviation * jax.random.normal(rng, shape, jnp.float32)
    if pieces:
        array = array * level_of(rng, shape, pieces, -0.22, 0.18)
    return jnp.clip(array, -most, most).astype(kind)


def noise_with(key, shape, scale, most, pieces, heavy, kind=jnp.bfloat16):
    drawn = scale * jax.random.normal(key, shape, jnp.float32)
    if pieces:
        drawn = drawn * level_of(key, shape, pieces, -0.22, 0.18)
    return jnp.clip(strengthened(drawn, jax.random.fold_in(key, 3), *heavy), -most, most).astype(kind)


def setup_inputs(seed: int = 0) -> dict:
    splits = jax.random.split(jax.random.key(seed), 11)
    return {
        "queries": draw_queries(jax.random.fold_in(splits[10], 71), 0),
        "keys": draw_keys(jax.random.fold_in(splits[10], 71), 0),
        "values": normal_values(splits[2], (TOKENS, HEADS * HD), 1.0, 6.0, ((0, 16), (1, 16))),
        "cross_queries": draw_cross_queries(jax.random.fold_in(splits[10], 71), 0),
        "history_keys": draw_history_keys(jax.random.fold_in(splits[10], 71), 0),
        "history_values": normal_values(splits[5], (HISTORY, HEADS * HD), 1.0, 6.0, ((0, 16), (1, 16))),
        "frame_ids": jnp.searchsorted(jnp.cumsum(uneven_parts(splits[6], FRAMES, TOKENS, FRAME_MOST, 1)), jnp.arange(TOKENS), side="right").astype(jnp.int32),
        "masked": place_ends((jax.random.randint(splits[7], (TOKENS,), 0, 2) < 1).astype(jnp.int32), jax.random.fold_in(splits[7], 1), 0, 1),
        "out_weight": normal_values(splits[8], (HEADS * HD, D), (HEADS * HD) ** -0.5, 0.09375, ((0, 16),)),
        "cotangent": noise_with(splits[9], (TOKENS, D), 1.0, 6.0, ((0, 16), (1, 16)), (0, 1, 16, 2.0)),
    }


def normalize(score):
    highest = jnp.max(score, axis=-1, keepdims=True)
    weights = jnp.exp(score - highest)
    return weights / jnp.sum(weights, axis=-1, keepdims=True)


def head_slice(matrix, head):
    return lax.dynamic_slice_in_dim(matrix, head * HD, HD, 1)


def head_probs(queries, keys, cross_queries, history_keys, allowed, head):
    factor = HD ** -0.5
    self_score = jnp.dot(head_slice(queries, head), head_slice(keys, head).T, preferred_element_type=jnp.float32) * factor
    self_prob = normalize(jnp.where(allowed, self_score, -jnp.inf))
    cross_score = jnp.dot(head_slice(cross_queries, head), head_slice(history_keys, head).T, preferred_element_type=jnp.float32) * factor
    return self_prob, normalize(cross_score)


def flatten(stacked):
    return jnp.transpose(stacked, (1, 0, 2)).reshape(stacked.shape[1], HEADS * HD)


def reference(queries, keys, values, cross_queries, history_keys, history_values, frame_ids, masked, out_weight, cotangent):
    factor = HD ** -0.5
    positions = jnp.arange(TOKENS, dtype=jnp.int32)
    causal = frame_ids[None, :] <= frame_ids[:, None]
    allowed = causal & ((masked[None, :] == 0) | (positions[None, :] == positions[:, None]))
    head_ids = jnp.arange(HEADS, dtype=jnp.int32)

    def forward_head(head):
        self_prob, cross_prob = head_probs(queries, keys, cross_queries, history_keys, allowed, head)
        self_out = jnp.dot(self_prob.astype(jnp.bfloat16), head_slice(values, head), preferred_element_type=jnp.float32)
        cross_out = jnp.dot(cross_prob.astype(jnp.bfloat16), head_slice(history_values, head), preferred_element_type=jnp.float32)
        return self_out + cross_out

    attended = flatten(lax.map(forward_head, head_ids)).astype(jnp.bfloat16)
    layer_out = jnp.dot(attended, out_weight, preferred_element_type=jnp.float32).astype(jnp.bfloat16)
    grad_attended = jnp.dot(cotangent, out_weight.T, preferred_element_type=jnp.float32).astype(jnp.bfloat16)
    weight_grad = jnp.dot(attended.T, cotangent, preferred_element_type=jnp.float32)

    def backward_head(head):
        self_prob, cross_prob = head_probs(queries, keys, cross_queries, history_keys, allowed, head)
        grad_head = head_slice(grad_attended, head)
        self_dprob = jnp.dot(grad_head, head_slice(values, head).T, preferred_element_type=jnp.float32)
        self_dot = jnp.sum(self_prob * self_dprob, axis=-1, keepdims=True)
        self_dscore = (self_prob * (self_dprob - self_dot)).astype(jnp.bfloat16)
        cross_dprob = jnp.dot(grad_head, head_slice(history_values, head).T, preferred_element_type=jnp.float32)
        cross_dot = jnp.sum(cross_prob * cross_dprob, axis=-1, keepdims=True)
        cross_dscore = (cross_prob * (cross_dprob - cross_dot)).astype(jnp.bfloat16)
        query_part = jnp.dot(self_dscore, head_slice(keys, head), preferred_element_type=jnp.float32) * factor
        key_part = jnp.dot(self_dscore.T, head_slice(queries, head), preferred_element_type=jnp.float32) * factor
        value_part = jnp.dot(self_prob.astype(jnp.bfloat16).T, grad_head, preferred_element_type=jnp.float32)
        cross_part = jnp.dot(cross_dscore, head_slice(history_keys, head), preferred_element_type=jnp.float32) * factor
        memory_part = jnp.dot(cross_dscore.T, head_slice(cross_queries, head), preferred_element_type=jnp.float32) * factor
        recall_part = jnp.dot(cross_prob.astype(jnp.bfloat16).T, grad_head, preferred_element_type=jnp.float32)
        return query_part, key_part, value_part, cross_part, memory_part, recall_part

    gradients = lax.map(backward_head, head_ids)
    query_grad, key_grad, value_grad, cross_query_grad, history_key_grad, history_value_grad = [flatten(member).astype(jnp.bfloat16) for member in gradients]
    return (layer_out, query_grad, key_grad, value_grad, cross_query_grad, history_key_grad, history_value_grad, weight_grad)
```

```python
import itertools

import jax
import jax.numpy as jnp
from jax import lax
from jax.experimental import pallas as pl
from jax.experimental.pallas import tpu as pltpu
from jax.sharding import Mesh
from jax.sharding import PartitionSpec as P

F32, BF16 = jnp.float32, jnp.bfloat16
HD = 128
FACTOR = HD**-0.5
NZ, NX = 8, 4
HIDDEN = -1e30
NEVER = 1e9
MESH = pl.DeviceIdType.MESH
AXES = ("yl", "z", "x", "core", "yh")
GRP, COLS = ("yl", "z"), ("x", "core", "yh")

K0, V0, HK0, HV0, KV_ROWS = 0, 256, 512, 896, 1280
OUT_AT = ((0, 128), (256, 128), (512, 128), (768, 128), (1024, 192), (1408, 192))
OUT_ROWS = 1792


def dot(a, b):
    return lax.dot_general(a, b, (((1,), (0,)), ((), ())), preferred_element_type=F32)


def dot_t(a, b):
    return lax.dot_general(a, b, (((1,), (1,)), ((), ())), preferred_element_type=F32)


def kernel(
    q, k, v, cq, hk, hv, w_hbm, cot, row, col,
    out, oq, ok, ov, ocq, ohk, ohv, att_all,
    kv, qs, gr, st, self_s, cross_s, m_s, l_s, acc_s, w, cot_in, cf, part, core_in,
    mid, x_in, y_out, y_in, grad_out, att_own, att_out, ka, dqa, xo, xi,
    send_sems, recv_sems, w_sem,
):
    yl, z, x = lax.axis_index("yl"), lax.axis_index("z"), lax.axis_index("x")
    core, yh = lax.axis_index("core"), lax.axis_index("yh")
    mate_y, mate_c, mate_h = {"yl": 1 - yl}, {"core": 1 - core}, {"yh": 1 - yh}

    def at_z(d):
        return lax.rem(z + (d + NZ), NZ)

    def at_x(d):
        return lax.rem(x + (d + NX), NX)

    peers = [mate_y, mate_c, mate_h]
    peers += [{"z": at_z(d)} for d in range(1, NZ)] + [{"x": at_x(d)} for d in range(1, NX)]
    barrier = pltpu.get_barrier_semaphore()
    for peer in peers:
        pl.semaphore_signal(barrier, inc=1, device_id=peer, device_id_type=MESH)
    w_copy = pltpu.make_async_copy(w_hbm, w, w_sem.at[0])
    w_copy.start()
    pl.semaphore_wait(barrier, len(peers))

    number = itertools.count()
    started = []

    def send(src, dst, to):
        i = next(number)
        copy = pltpu.make_async_remote_copy(
            src_ref=src, dst_ref=dst, send_sem=send_sems.at[i], recv_sem=recv_sems.at[i],
            device_id=to, device_id_type=MESH,
        )
        copy.start()
        started.append(copy)
        return copy

    def lanes(i):
        return pl.ds(pl.multiple_of(i * HD, HD), HD)

    def rows(base, i, n):
        return pl.ds(pl.multiple_of(base + i * n, 16), n)

    owned = ((k, kv, K0, 128), (hk, kv, HK0, 192), (v, kv, V0, 128), (hv, kv, HV0, 192), (q, qs, 0, 128), (cq, qs, 256, 128))
    cot_copy = send(cot, cot_in, mate_h)
    swaps = [
        send(src.at[:, lanes(1 - yl)], dst.at[z, rows(base, yl, n)], mate_y)
        for src, dst, base, n in owned
    ]
    for src, dst, base, n in owned:
        dst[z, rows(base, yl, n), :] = src[:, lanes(yl)]

    def ring_step(ref, s, before):
        for copy in before:
            copy.wait_recv()
        right, left = {"z": at_z(1)}, {"z": at_z(-1)}
        from_r, from_l = at_z(-s), at_z(s)
        if s < NZ // 2 - 1:
            return [
                send(ref.at[from_r], ref.at[from_r], right),
                send(ref.at[from_l], ref.at[from_l], left),
            ]
        half = ref.shape[1] // 2
        return [
            send(ref.at[from_r, pl.ds(0, half)], ref.at[from_r, pl.ds(0, half)], right),
            send(ref.at[from_l, pl.ds(half, half)], ref.at[from_l, pl.ds(half, half)], left),
        ]

    def wait_all(copies):
        for copy in copies:
            copy.wait_recv()

    m_s[...] = jnp.full(m_s.shape, HIDDEN, F32)
    l_s[...] = jnp.zeros(l_s.shape, F32)
    acc_s[...] = jnp.zeros(acc_s.shape, F32)

    def take_in(i, s, values):
        top = m_s[i]
        new = jnp.maximum(top, jnp.max(s, axis=1, keepdims=True))
        p = jnp.exp(s - new)
        shrink = jnp.exp(top - new)
        l_s[i] = l_s[i] * shrink + jnp.sum(p, axis=1, keepdims=True)
        acc_s[i] = acc_s[i] * shrink + dot(p.astype(BF16), values)
        m_s[i] = new

    def attend(o):
        s = dot_t(qs[z, 0:256, :], kv[o, K0 : K0 + 256, :]) * FACTOR
        keep = (row[o, 1:2, :] <= col[:, 0:1]) | (row[o, 2:3, :] == col[:, 2:3])
        s = jnp.where(keep, s, HIDDEN)
        self_s[o] = s
        take_in(0, s, kv[o, V0 : V0 + 256, :])
        s = dot_t(qs[z, 256:512, :], kv[o, HK0 : HK0 + 384, :]) * FACTOR
        cross_s[o] = s
        take_in(1, s, kv[o, HV0 : HV0 + 384, :])

    def attend_both(d):
        def body(i, carry):
            attend(lax.rem(z + NZ + d * (1 - 2 * i), NZ))
            return carry

        lax.fori_loop(0, 2, body, 0)

    wait_all(swaps[0:4])
    a0 = ring_step(kv, 0, [])
    wait_all(swaps[4:6])
    b0 = ring_step(qs, 0, [])

    cot_copy.wait_recv()
    mine = x * 2 + core

    @pl.when(yh == 0)
    def _():
        cf[mine] = jnp.concatenate([cot[...], cot_in[...]], axis=1)

    @pl.when(yh == 1)
    def _():
        cf[mine] = jnp.concatenate([cot_in[...], cot[...]], axis=1)

    def slot(d):
        return at_x(d) * 2 + core

    c_right = send(cf.at[mine], cf.at[mine], {"x": at_x(1)})
    c_left = send(cf.at[mine], cf.at[mine], {"x": at_x(-1)})
    c_core = [send(cf.at[mine], cf.at[mine], mate_c)]

    attend(z)

    c_right.wait_recv()
    c_right2 = send(cf.at[slot(-1), pl.ds(0, 64)], cf.at[slot(-1), pl.ds(0, 64)], {"x": at_x(1)})
    c_core.append(send(cf.at[slot(-1)], cf.at[slot(-1)], mate_c))
    c_left.wait_recv()
    c_left2 = send(cf.at[slot(1), pl.ds(64, 64)], cf.at[slot(1), pl.ds(64, 64)], {"x": at_x(-1)})
    c_core.append(send(cf.at[slot(1)], cf.at[slot(1)], mate_c))
    a1 = ring_step(kv, 1, a0)
    attend_both(1)
    c_right2.wait_recv()
    c_left2.wait_recv()
    c_core.append(send(cf.at[slot(2)], cf.at[slot(2)], mate_c))
    a2 = ring_step(kv, 2, a1)
    b1 = ring_step(qs, 1, b0)

    wait_all(c_core)
    w_copy.wait()
    grad = dot_t(cf[0], w[:, 0:640])
    for b in range(1, 8):
        grad = grad + dot_t(cf[b], w[:, 640 * b : 640 * (b + 1)])
    grad_out[...] = grad.astype(BF16)
    g_swap = send(grad_out.at[:, lanes(1 - yl)], gr.at[z, rows(0, yl, 128)], mate_y)
    gr[z, rows(0, yl, 128), :] = grad_out[:, lanes(yl)]

    attend_both(2)
    a3 = ring_step(kv, 3, a2)
    b2 = ring_step(qs, 2, b1)
    g_swap.wait_recv()
    g0 = ring_step(gr, 0, [])
    attend_both(3)
    wait_all(a3)
    attend(at_z(4))

    heads = [acc_s[i] / l_s[i] for i in range(2)]
    logs = [m_s[i] + jnp.log(l_s[i]) for i in range(2)]
    att = (heads[0] + heads[1]).astype(BF16)
    att_out[...] = att
    t_swap = send(att_out, att_own.at[1], mate_y)
    g_own = gr[z].astype(F32)
    dots = [jnp.sum(g_own * heads[i], axis=1, keepdims=True) for i in range(2)]
    lane = lax.broadcasted_iota(jnp.int32, (256, HD), 1)
    table = jnp.zeros((256, HD), F32)
    for i, column in enumerate(logs + dots):
        table = jnp.where(lane == i, column, table)
    st[z] = table.T[0:8, :]
    s_copies = [send(st.at[z], st.at[z], {"z": at_z(d)}) for d in range(1, NZ)]
    b3 = ring_step(qs, 3, b2)
    g1 = ring_step(gr, 1, g0)

    t_swap.wait_recv()
    for half in range(2):
        a_rows = pl.ds(half * 128, 128)
        att_all[half, z, :, lanes(yl)] = att_out[a_rows, :]
        att_all[half, z, :, lanes(1 - yl)] = att_own[1, a_rows, :]

    def att_step(s, before):
        wait_all(before)
        right, left = {"z": at_z(1)}, {"z": at_z(-1)}
        from_r, from_l = at_z(-s), at_z(s)
        last = s == NZ // 2 - 1
        made = []
        for half in range(2):
            if not (last and half == 1):
                made.append(send(att_all.at[half, from_r], att_all.at[half, from_r], right))
            if not (last and half == 0):
                made.append(send(att_all.at[half, from_l], att_all.at[half, from_l], left))
        return made

    t0 = att_step(0, [])

    own_att = att_all[yl, z]
    for b in range(8):
        part[b] = dot(own_att, w[:, 640 * b : 640 * (b + 1)]).astype(BF16)
    p_core = [
        send(part.at[2 * i + (1 - core)], core_in.at[i], mate_c) for i in range(NX)
    ]

    def query_side(o, carry):
        g = gr[z]
        p = jnp.exp(self_s[o] - logs[0])
        d = dot_t(g, kv[o, V0 : V0 + 256, :])
        ds = (p * (d - dots[0])).astype(BF16)
        dqa[0] += dot(ds, kv[o, K0 : K0 + 256, :])
        p = jnp.exp(cross_s[o] - logs[1])
        d = dot_t(g, kv[o, HV0 : HV0 + 384, :])
        ds = (p * (d - dots[1])).astype(BF16)
        dqa[1] += dot(ds, kv[o, HK0 : HK0 + 384, :])
        return carry

    dqa[...] = jnp.zeros(dqa.shape, F32)
    lax.fori_loop(0, 4, query_side, 0)

    wait_all(p_core)

    def add_cores(i, carry):
        both = part[2 * i + core].astype(F32) + core_in[i].astype(F32)
        mid[i] = both.astype(BF16)
        return carry

    lax.fori_loop(0, NX, add_cores, 0)
    p_x = [send(mid.at[at_x(d)], x_in.at[d - 1], {"x": at_x(d)}) for d in (1, 3, 2)]
    g2 = ring_step(gr, 2, g1)
    t1 = att_step(1, t0)

    lax.fori_loop(4, 8, query_side, 0)
    g3 = ring_step(gr, 3, g2)
    t2 = att_step(2, t1)

    def give_back(i, values):
        base, n = OUT_AT[i]
        xo[base : base + 2 * n, :] = values.astype(BF16)
        at = rows(base, 1 - yl, n)
        return send(xo.at[at], xi.at[at], mate_y)

    backs = [(oq, 0, give_back(0, dqa[0] * FACTOR)), (ocq, 1, give_back(1, dqa[1] * FACTOR))]

    wait_all(s_copies)
    ka[...] = jnp.zeros(ka.shape, F32)

    def key_side(o):
        g = gr[o]
        keep = (col[:, 1:2] <= row[o, 0:1, :]) | (col[:, 2:3] == row[o, 2:3, :])
        s = jnp.where(keep, dot_t(kv[z, K0 : K0 + 256, :], qs[o, 0:256, :]) * FACTOR, HIDDEN)
        for qq, stat, at_k, at_v, n in ((qs[o, 0:256, :], 0, K0, V0, 256), (qs[o, 256:512, :], 1, HK0, HV0, 384)):
            if stat == 1:
                s = dot_t(kv[z, at_k : at_k + n, :], qq) * FACTOR
            p = jnp.exp(s - st[o, stat : stat + 1, :])
            ka[at_v : at_v + n, :] += dot(p.astype(BF16), g)
            d = dot_t(kv[z, at_v : at_v + n, :], g)
            ds = (p * (d - st[o, stat + 2 : stat + 3, :])).astype(BF16)
            ka[at_k : at_k + n, :] += dot(ds, qq)

    def keys_both(first, count):
        def body(i, carry):
            d = first + lax.div(i, 2)
            sign = 1 - 2 * lax.rem(i, 2)
            key_side(lax.rem(z + NZ + d * sign, NZ))
            return carry

        lax.fori_loop(0, 2 * count, body, 0)

    key_side(z)
    keys_both(1, 2)

    wait_all(p_x)
    total = mid[x].astype(F32)
    for d in range(3):
        total = total + x_in[d].astype(F32)

    @pl.when(yh == 0)
    def _():
        y_out[0] = total[:, 0:320]
        y_out[1] = total[:, 320:640]

    @pl.when(yh == 1)
    def _():
        y_out[0] = total[:, 320:640]
        y_out[1] = total[:, 0:320]

    y_in[0] = y_out[1].astype(BF16)
    p_y = send(y_in.at[0], y_in.at[1], mate_h)

    wait_all(b3)
    t3 = att_step(3, t2)
    keys_both(3, 1)
    wait_all(g3)
    key_side(at_z(4))

    for i, ref, base, n, scale in ((2, ok, K0, 256, FACTOR), (3, ov, V0, 256, 1.0), (4, ohk, HK0, 384, FACTOR), (5, ohv, HV0, 384, 1.0)):
        backs.append((ref, i, give_back(i, ka[base : base + n, :] * scale)))

    p_y.wait_recv()
    out[...] = (y_out[0] + y_in[1].astype(F32)).astype(BF16)
    for ref, i, copy in backs:
        base, n = OUT_AT[i]
        copy.wait_recv()
        ref[:, lanes(yl)] = xo[rows(base, yl, n), :]
        ref[:, lanes(1 - yl)] = xi[rows(base, yl, n), :]
    wait_all(t3)
    for copy in started:
        copy.wait_send()


def on_device(q, k, v, cq, hk, hv, frame_ids, masked, w, cot):
    z = lax.axis_index("z")
    frames = frame_ids.astype(F32)
    key_frames = jnp.where(masked == 0, frames, NEVER)
    place = jnp.arange(frames.shape[0], dtype=jnp.int32).astype(F32)

    def by_z(a):
        return a.reshape(2, NZ, 128).transpose(1, 0, 2).reshape(NZ, 256)

    info = jnp.stack([by_z(frames), by_z(key_frames), by_z(place)], axis=1)
    row = jnp.pad(info, ((0, 0), (0, 5), (0, 0)))
    own = lax.dynamic_index_in_dim(info, z, 0, keepdims=False)
    col = jnp.pad(own.T, ((0, 0), (0, HD - 3)))

    swap = [(i, (i % 16) * 16 + i // 16) for i in range(256)]
    turned = lax.ppermute(cot, AXES, swap)
    tall = lax.all_gather(turned, COLS, axis=0, tiled=True)

    vmem = pl.BlockSpec(memory_space=pltpu.VMEM)
    shape = jax.ShapeDtypeStruct
    results = pl.pallas_call(
        kernel,
        out_shape=(
            shape((128, 320), BF16),
            *[shape((128, 256), BF16)] * 4,
            *[shape((192, 256), BF16)] * 2,
            shape((2, NZ, 128, 256), BF16),
        ),
        in_specs=[vmem] * 6 + [pl.BlockSpec(memory_space=pl.ANY)] + [vmem] * 3,
        out_specs=[vmem] * 8,
        scratch_shapes=[
            pltpu.VMEM((NZ, KV_ROWS, HD), BF16),
            pltpu.VMEM((NZ, 512, HD), BF16),
            pltpu.VMEM((NZ, 256, HD), BF16),
            pltpu.VMEM((NZ, 8, 256), F32),
            pltpu.VMEM((NZ, 256, 256), F32),
            pltpu.VMEM((NZ, 256, 384), F32),
            pltpu.VMEM((2, 256, 1), F32),
            pltpu.VMEM((2, 256, 1), F32),
            pltpu.VMEM((2, 256, HD), F32),
            pltpu.VMEM((256, 5120), BF16),
            pltpu.VMEM((128, 320), BF16),
            pltpu.VMEM((8, 128, 640), BF16),
            pltpu.VMEM((8, 128, 640), BF16),
            pltpu.VMEM((NX, 128, 640), BF16),
            pltpu.VMEM((NX, 128, 640), BF16),
            pltpu.VMEM((NX - 1, 128, 640), BF16),
            pltpu.VMEM((2, 128, 320), F32),
            pltpu.VMEM((2, 128, 320), BF16),
            pltpu.VMEM((128, 256), BF16),
            pltpu.VMEM((2, 256, HD), BF16),
            pltpu.VMEM((256, HD), BF16),
            pltpu.VMEM((KV_ROWS, HD), F32),
            pltpu.VMEM((2, 256, HD), F32),
            pltpu.VMEM((OUT_ROWS, HD), BF16),
            pltpu.VMEM((OUT_ROWS, HD), BF16),
            pltpu.SemaphoreType.DMA((96,)),
            pltpu.SemaphoreType.DMA((96,)),
            pltpu.SemaphoreType.DMA((1,)),
        ],
        compiler_params=pltpu.CompilerParams(
            collective_id=0, has_side_effects=True, vmem_limit_bytes=50 * 2**20
        ),
        cost_estimate=pl.CostEstimate(
            flops=4_000_000_000, bytes_accessed=10_000_000, transcendentals=3_000_000
        ),
    )(q, k, v, cq, hk, hv, w, cot, row, col)
    att = results[7].reshape(2048, 256)
    weight_grad = lax.dot_general(
        att, tall, (((0,), (0,)), ((), ())), preferred_element_type=F32
    )
    return (*results[:7], weight_grad)


def solution(mesh):
    finer = Mesh(mesh.devices.reshape(2, NZ, NX, 2, 2), AXES)
    split = P(GRP, COLS)
    return jax.shard_map(
        on_device,
        mesh=finer,
        in_specs=(*[split] * 6, P(), P(), P(COLS, None), split),
        out_specs=(*[split] * 7, P(COLS, GRP)),
        check_vma=False,
    )
```

```python
import itertools

import jax
import jax.numpy as jnp
from jax import lax
from jax.experimental import pallas as pl
from jax.experimental.pallas import tpu as pltpu
from jax.sharding import Mesh
from jax.sharding import PartitionSpec as P

F32, BF16 = jnp.float32, jnp.bfloat16
HD = 128
FACTOR = HD**-0.5
NZ, NX = 8, 4
HIDDEN = -1e30
NEVER = 1e9
MESH = pl.DeviceIdType.MESH
AXES = ("yl", "z", "x", "core", "yh")
GRP, COLS = ("yl", "z"), ("x", "core", "yh")

K0, V0, HK0, HV0, KV_ROWS = 0, 256, 512, 896, 1280
OUT_AT = ((0, 128), (256, 128), (512, 128), (768, 128), (1024, 192), (1408, 192))
OUT_ROWS = 1792
TURN, TURN_OWN = 127, 31


def dot(a, b):
    return lax.dot_general(a, b, (((1,), (0,)), ((), ())), preferred_element_type=F32)


def dot_t(a, b):
    return lax.dot_general(a, b, (((1,), (1,)), ((), ())), preferred_element_type=F32)


def kernel(
    q, k, v, cq, hk, hv, w_hbm, cot, frames, masked,
    out_h, oq_h, ok_h, ov_h, ocq_h, ohk_h, ohv_h, wg_h,
    out, oq, ok, ov, ocq, ohk, ohv, wg, att_all, tall, kv, qs, gr, st, self_s, cross_s, m_s, l_s, acc_s, w, cf, part, core_in,
    mid, x_in, y_out, y_in, grad_out, ka, dqa, xo, xi, row_q, row_k, row_p, col,
    send_sems, recv_sems, own_sems,
):
    yl, z, x = lax.axis_index("yl"), lax.axis_index("z"), lax.axis_index("x")
    core, yh = lax.axis_index("core"), lax.axis_index("yh")
    mate_y, mate_c, mate_h = {"yl": 1 - yl}, {"core": 1 - core}, {"yh": 1 - yh}
    blk = x * 2 + core
    tokens, chunk = yl * NZ + z, blk * 2 + yh
    turned = {
        "yl": lax.div(chunk, NZ), "z": lax.rem(chunk, NZ), "x": lax.div(tokens, 4),
        "core": lax.rem(lax.div(tokens, 2), 2), "yh": lax.rem(tokens, 2),
    }

    def at_z(d):
        return lax.rem(z + (d + NZ), NZ)

    def at_x(d):
        return lax.rem(x + (d + NX), NX)

    peers = [mate_y, mate_c, mate_h]
    peers += [{"z": at_z(d)} for d in range(1, NZ)] + [{"x": at_x(d)} for d in range(1, NX)]
    barrier = pltpu.get_barrier_semaphore()
    for peer in peers:
        pl.semaphore_signal(barrier, inc=1, device_id=peer, device_id_type=MESH)

    @pl.when(tokens != chunk)
    def _():
        pl.semaphore_signal(barrier, inc=1, device_id=turned, device_id_type=MESH)

    own_number = itertools.count()

    def bring(src, dst):
        copy = pltpu.make_async_copy(src, dst, own_sems.at[next(own_number)])
        copy.start()
        return copy

    def lanes(i):
        return pl.ds(pl.multiple_of(i * HD, HD), HD)

    def rows(base, i, n):
        return pl.ds(pl.multiple_of(base + i * n, 16), n)

    owned = ((k, kv, K0, 128), (hk, kv, HK0, 192), (v, kv, V0, 128), (hv, kv, HV0, 192), (q, qs, 0, 128), (cq, qs, 256, 128))
    brought = [bring(src.at[:, lanes(yl)], dst.at[z, rows(base, yl, n)]) for src, dst, base, n in owned]
    cot_own = bring(cot, cf.at[chunk])
    w_copy = bring(w_hbm, w)
    pl.semaphore_wait(barrier, len(peers) + (tokens != chunk).astype(jnp.int32))

    number = itertools.count()
    started = []

    def send(src, dst, to):
        i = next(number)
        copy = pltpu.make_async_remote_copy(
            src_ref=src, dst_ref=dst, send_sem=send_sems.at[i], recv_sem=recv_sems.at[i],
            device_id=to, device_id_type=MESH,
        )
        copy.start()
        started.append(copy)
        return copy

    cot_copy = send(cot, cf.at[chunk], mate_h)
    swaps = [
        send(src.at[:, lanes(1 - yl)], dst.at[z, rows(base, yl, n)], mate_y)
        for src, dst, base, n in owned
    ]
    t_copy = pltpu.make_async_remote_copy(
        src_ref=cot, dst_ref=tall.at[tokens], send_sem=send_sems.at[TURN], recv_sem=recv_sems.at[TURN],
        device_id=turned, device_id_type=MESH,
    )
    t_own = pltpu.make_async_copy(cot, tall.at[tokens], own_sems.at[TURN_OWN])

    @pl.when(tokens != chunk)
    def _():
        t_copy.start()

    @pl.when(tokens == chunk)
    def _():
        t_own.start()

    lane = lax.broadcasted_iota(jnp.int32, (NZ, 256), 1)
    place = lax.broadcasted_iota(jnp.int32, (NZ, 256), 0) * 128 + lane
    place = jnp.where(lane < 128, place, place + (NZ * 128 - 128))
    row_p[...] = place.astype(F32)
    own_frames = frames[...].astype(F32)
    key_frames = jnp.where(masked[...] == 0, own_frames, NEVER)
    row_q[...] = jnp.concatenate([own_frames[0:NZ], own_frames[NZ : 2 * NZ]], axis=1)
    row_k[...] = jnp.concatenate([key_frames[0:NZ], key_frames[NZ : 2 * NZ]], axis=1)
    which = lax.broadcasted_iota(jnp.int32, (HD, 256), 0)
    spread = jnp.where(which == 0, row_q[pl.ds(z, 1), :], row_k[pl.ds(z, 1), :])
    col[...] = jnp.where(which == 2, row_p[pl.ds(z, 1), :], spread).T

    def ring_step(view, s, before):
        for copy in before:
            copy.wait_recv()
        right, left = {"z": at_z(1)}, {"z": at_z(-1)}
        last = s == NZ // 2 - 1
        from_r, from_l = view(at_z(-s), 0 if last else None), view(at_z(s), 1 if last else None)
        return [send(from_r, from_r, right), send(from_l, from_l, left)]

    def whole_or_half(ref):
        half = ref.shape[1] // 2

        def view(o, part):
            return ref.at[o] if part is None else ref.at[o, pl.ds(part * half, half)]

        return view

    kv_view, qs_view, gr_view = whole_or_half(kv), whole_or_half(qs), whole_or_half(gr)

    def att_view(o, part):
        return att_all.at[slice(None) if part is None else part, o, :, lanes(yl)]

    def wait_all(copies):
        for copy in copies:
            copy.wait_recv()

    m_s[...] = jnp.full(m_s.shape, HIDDEN, F32)
    l_s[...] = jnp.zeros(l_s.shape, F32)
    acc_s[...] = jnp.zeros(acc_s.shape, F32)

    def take_in(i, s, values):
        top = m_s[i]
        new = jnp.maximum(top, jnp.max(s, axis=1, keepdims=True))
        p = jnp.exp(s - new)
        shrink = jnp.exp(top - new)
        l_s[i] = l_s[i] * shrink + jnp.sum(p, axis=1, keepdims=True)
        acc_s[i] = acc_s[i] * shrink + dot(p.astype(BF16), values)
        m_s[i] = new

    def attend(o):
        s = dot_t(qs[z, 0:256, :], kv[o, K0 : K0 + 256, :]) * FACTOR
        keep = (row_k[pl.ds(o, 1), :] <= col[:, 0:1]) | (row_p[pl.ds(o, 1), :] == col[:, 2:3])
        s = jnp.where(keep, s, HIDDEN)
        self_s[o] = s
        take_in(0, s, kv[o, V0 : V0 + 256, :])
        s = dot_t(qs[z, 256:512, :], kv[o, HK0 : HK0 + 384, :]) * FACTOR
        cross_s[o] = s
        take_in(1, s, kv[o, HV0 : HV0 + 384, :])

    def attend_both(d):
        def body(i, carry):
            attend(lax.rem(z + NZ + d * (1 - 2 * i), NZ))
            return carry

        lax.fori_loop(0, 2, body, 0)

    for copy in brought[0:4]:
        copy.wait()
    wait_all(swaps[0:4])
    a0 = ring_step(kv_view, 0, [])
    for copy in brought[4:6]:
        copy.wait()
    wait_all(swaps[4:6])
    b0 = ring_step(qs_view, 0, [])

    def pair(ref, d):
        return ref.at[pl.ds((at_x(d) * 2 + core) * 2, 2)]

    def one(ref, d, i):
        return ref.at[(at_x(d) * 2 + core) * 2 + i]

    def x_first(ref):
        mine = pair(ref, 0)
        return [send(mine, mine, {"x": at_x(1)}), send(mine, mine, {"x": at_x(-1)}), send(mine, mine, mate_c)]

    def x_second(ref, before):
        before[0].wait_recv()
        far = one(ref, -1, 0)
        made = [send(far, far, {"x": at_x(1)})]
        cores = [before[2], send(pair(ref, -1), pair(ref, -1), mate_c)]
        before[1].wait_recv()
        far = one(ref, 1, 1)
        made.append(send(far, far, {"x": at_x(-1)}))
        cores.append(send(pair(ref, 1), pair(ref, 1), mate_c))
        return made, cores

    def x_third(ref, before):
        made, cores = before
        wait_all(made)
        return cores + [send(pair(ref, 2), pair(ref, 2), mate_c)]

    cot_own.wait()
    cot_copy.wait_recv()
    c_first = x_first(cf)
    attend(z)
    c_second = x_second(cf, c_first)
    a1 = ring_step(kv_view, 1, a0)

    @pl.when(tokens != chunk)
    def _():
        t_copy.wait()

    @pl.when(tokens == chunk)
    def _():
        t_own.wait()

    turn_h = send(tall.at[chunk], tall.at[chunk], mate_h)
    attend_both(1)
    c_core = x_third(cf, c_second)
    a2 = ring_step(kv_view, 2, a1)
    b1 = ring_step(qs_view, 1, b0)
    turn_h.wait_recv()
    turn_first = x_first(tall)

    wait_all(c_core)
    w_copy.wait()
    grad = dot(w[:, 0:640], cf[0:2].reshape(640, HD))
    for b in range(1, 8):
        grad = grad + dot(w[:, 640 * b : 640 * (b + 1)], cf[2 * b : 2 * b + 2].reshape(640, HD))
    grad_out[...] = grad.T.astype(BF16)
    g_swap = send(grad_out.at[:, lanes(1 - yl)], gr.at[z, rows(0, yl, 128)], mate_y)
    gr[z, rows(0, yl, 128), :] = grad_out[:, lanes(yl)]

    attend_both(2)
    a3 = ring_step(kv_view, 3, a2)
    b2 = ring_step(qs_view, 2, b1)
    g_swap.wait_recv()
    g0 = ring_step(gr_view, 0, [])
    turn_second = x_second(tall, turn_first)
    attend_both(3)
    wait_all(a3)
    attend(at_z(4))

    heads = [acc_s[i] / l_s[i] for i in range(2)]
    logs = [m_s[i] + jnp.log(l_s[i]) for i in range(2)]
    att = (heads[0] + heads[1]).astype(BF16)
    for half in range(2):
        att_all[half, z, :, lanes(yl)] = att[half * 128 : half * 128 + 128]

    def to_mate(o):
        return send(att_view(o, None), att_view(o, None), mate_y)

    t_mate = [to_mate(z)]
    g_own = gr[z].astype(F32)
    dots = [jnp.sum(g_own * heads[i], axis=1, keepdims=True) for i in range(2)]
    lane = lax.broadcasted_iota(jnp.int32, (256, HD), 1)
    table = jnp.zeros((256, HD), F32)
    for i, column in enumerate(logs + dots):
        table = jnp.where(lane == i, column, table)
    st[z] = table.T[0:8, :]
    s_copies = [send(st.at[z], st.at[z], {"z": at_z(d)}) for d in range(1, NZ)]
    b3 = ring_step(qs_view, 3, b2)
    g1 = ring_step(gr_view, 1, g0)

    t0 = ring_step(att_view, 0, [])
    turn_core = x_third(tall, turn_second)
    t_mate[0].wait_recv()

    own_att = att_all[yl, z]
    for b in range(8):
        part[b] = dot(own_att, w[:, 640 * b : 640 * (b + 1)]).astype(BF16)
    p_core = [
        send(part.at[2 * i + (1 - core)], core_in.at[i], mate_c) for i in range(NX)
    ]

    def query_side(o, carry):
        g = gr[z]
        p = jnp.exp(self_s[o] - logs[0])
        d = dot_t(g, kv[o, V0 : V0 + 256, :])
        ds = (p * (d - dots[0])).astype(BF16)
        dqa[0] += dot(ds, kv[o, K0 : K0 + 256, :])
        p = jnp.exp(cross_s[o] - logs[1])
        d = dot_t(g, kv[o, HV0 : HV0 + 384, :])
        ds = (p * (d - dots[1])).astype(BF16)
        dqa[1] += dot(ds, kv[o, HK0 : HK0 + 384, :])
        return carry

    dqa[...] = jnp.zeros(dqa.shape, F32)
    lax.fori_loop(0, 4, query_side, 0)

    wait_all(p_core)

    def add_cores(i, carry):
        both = part[2 * i + core].astype(F32) + core_in[i].astype(F32)
        mid[i] = both.astype(BF16)
        return carry

    lax.fori_loop(0, NX, add_cores, 0)
    p_x = [send(mid.at[at_x(d)], x_in.at[d - 1], {"x": at_x(d)}) for d in (1, 3, 2)]
    g2 = ring_step(gr_view, 2, g1)
    t1 = ring_step(att_view, 1, t0)
    t_mate += [to_mate(at_z(1)), to_mate(at_z(-1))]

    lax.fori_loop(4, 8, query_side, 0)
    g3 = ring_step(gr_view, 3, g2)
    t2 = ring_step(att_view, 2, t1)
    t_mate += [to_mate(at_z(2)), to_mate(at_z(-2))]

    def give_back(i, values):
        base, n = OUT_AT[i]
        xo[base : base + 2 * n, :] = values.astype(BF16)
        at = rows(base, 1 - yl, n)
        return send(xo.at[at], xi.at[at], mate_y)

    backs = [(oq, 0, give_back(0, dqa[0] * FACTOR)), (ocq, 1, give_back(1, dqa[1] * FACTOR))]

    wait_all(s_copies)
    ka[...] = jnp.zeros(ka.shape, F32)

    def key_side(o):
        g = gr[o]
        keep = (col[:, 1:2] <= row_q[pl.ds(o, 1), :]) | (col[:, 2:3] == row_p[pl.ds(o, 1), :])
        s = jnp.where(keep, dot_t(kv[z, K0 : K0 + 256, :], qs[o, 0:256, :]) * FACTOR, HIDDEN)
        for qq, stat, at_k, at_v, n in ((qs[o, 0:256, :], 0, K0, V0, 256), (qs[o, 256:512, :], 1, HK0, HV0, 384)):
            if stat == 1:
                s = dot_t(kv[z, at_k : at_k + n, :], qq) * FACTOR
            p = jnp.exp(s - st[o, stat : stat + 1, :])
            ka[at_v : at_v + n, :] += dot(p.astype(BF16), g)
            d = dot_t(kv[z, at_v : at_v + n, :], g)
            ds = (p * (d - st[o, stat + 2 : stat + 3, :])).astype(BF16)
            ka[at_k : at_k + n, :] += dot(ds, qq)

    def keys_both(first, count):
        def body(i, carry):
            d = first + lax.div(i, 2)
            sign = 1 - 2 * lax.rem(i, 2)
            key_side(lax.rem(z + NZ + d * sign, NZ))
            return carry

        lax.fori_loop(0, 2 * count, body, 0)

    key_side(z)
    keys_both(1, 2)

    wait_all(p_x)
    total = mid[x].astype(F32)
    for d in range(3):
        total = total + x_in[d].astype(F32)
    y_out[...] = total.T
    y_in[0] = y_out[pl.ds(pl.multiple_of((1 - yh) * 320, 64), 320), :].astype(BF16)
    p_y = send(y_in.at[0], y_in.at[1], mate_h)

    wait_all(b3)
    t3 = ring_step(att_view, 3, t2)
    t_mate += [to_mate(at_z(3)), to_mate(at_z(-3))]
    keys_both(3, 1)
    wait_all(t3)
    t_mate.append(to_mate(at_z(4)))
    wait_all(g3)
    key_side(at_z(4))

    for i, ref, base, n, scale in ((2, ok, K0, 256, FACTOR), (3, ov, V0, 256, 1.0), (4, ohk, HK0, 384, FACTOR), (5, ohv, HV0, 384, 1.0)):
        backs.append((ref, i, give_back(i, ka[base : base + n, :] * scale)))

    p_y.wait_recv()
    own_total = y_out[pl.ds(pl.multiple_of(yh * 320, 64), 320), :]
    out[...] = (own_total + y_in[1].astype(F32)).astype(BF16)
    leaving = [bring(out, out_h)]
    for (ref, i, copy), away in zip(backs, (oq_h, ocq_h, ok_h, ov_h, ohk_h, ohv_h)):
        base, n = OUT_AT[i]
        copy.wait_recv()
        ref[:, lanes(yl)] = xo[rows(base, yl, n), :]
        ref[:, lanes(1 - yl)] = xi[rows(base, yl, n), :]
        leaving.append(bring(ref, away))
    wait_all(turn_core)
    wait_all(t_mate[1:])
    total = jnp.zeros((320, 256), F32)
    for half in range(2):
        for o in range(NZ):
            total = total + dot(tall[half * NZ + o], att_all[half, o])
    wg[...] = total
    leaving.append(bring(wg, wg_h))
    for copy in started:
        copy.wait_send()
    for copy in leaving:
        copy.wait()


def finish(*refs):
    sources, outs, held, sems = refs[0:8], refs[8:16], refs[16:24], refs[24]
    inward = [pltpu.make_async_copy(s, h, sems.at[i]) for i, (s, h) in enumerate(zip(sources, held))]
    outward = [pltpu.make_async_copy(h, o, sems.at[8 + i]) for i, (h, o) in enumerate(zip(held, outs))]
    for copy in inward:
        copy.start()
    for copy, onward in zip(inward, outward):
        copy.wait()
        onward.start()
    for copy in outward:
        copy.wait()


def on_device(q, k, v, cq, hk, hv, frame_ids, masked, w, cot):
    vmem = pl.BlockSpec(memory_space=pltpu.VMEM)
    shape = jax.ShapeDtypeStruct
    away = pl.BlockSpec(memory_space=pl.ANY)
    kinds = (shape((320, 128), BF16), *[shape((128, 256), BF16)] * 4, *[shape((192, 256), BF16)] * 2, shape((320, 256), F32))
    results = pl.pallas_call(
        kernel,
        out_shape=kinds,
        in_specs=[away] * 8 + [vmem] * 2,
        out_specs=[away] * 8,
        scratch_shapes=[
            *[pltpu.VMEM(kind.shape, kind.dtype) for kind in kinds],
            pltpu.VMEM((2, NZ, 128, 256), BF16),
            pltpu.VMEM((2 * NZ, 320, HD), BF16),
            pltpu.VMEM((NZ, KV_ROWS, HD), BF16),
            pltpu.VMEM((NZ, 512, HD), BF16),
            pltpu.VMEM((NZ, 256, HD), BF16),
            pltpu.VMEM((NZ, 8, 256), F32),
            pltpu.VMEM((NZ, 256, 256), F32),
            pltpu.VMEM((NZ, 256, 384), F32),
            pltpu.VMEM((2, 256, 1), F32),
            pltpu.VMEM((2, 256, 1), F32),
            pltpu.VMEM((2, 256, HD), F32),
            pltpu.VMEM((256, 5120), BF16),
            pltpu.VMEM((16, 320, HD), BF16),
            pltpu.VMEM((8, 128, 640), BF16),
            pltpu.VMEM((NX, 128, 640), BF16),
            pltpu.VMEM((NX, 128, 640), BF16),
            pltpu.VMEM((NX - 1, 128, 640), BF16),
            pltpu.VMEM((640, HD), F32),
            pltpu.VMEM((2, 320, HD), BF16),
            pltpu.VMEM((128, 256), BF16),
            pltpu.VMEM((KV_ROWS, HD), F32),
            pltpu.VMEM((2, 256, HD), F32),
            pltpu.VMEM((OUT_ROWS, HD), BF16),
            pltpu.VMEM((OUT_ROWS, HD), BF16),
            *[pltpu.VMEM((NZ, 256), F32)] * 3,
            pltpu.VMEM((256, HD), F32),
            pltpu.SemaphoreType.DMA((TURN + 1,)),
            pltpu.SemaphoreType.DMA((TURN + 1,)),
            pltpu.SemaphoreType.DMA((TURN_OWN + 1,)),
        ],
        compiler_params=pltpu.CompilerParams(
            collective_id=0, has_side_effects=True, vmem_limit_bytes=60 * 2**20
        ),
        cost_estimate=pl.CostEstimate(
            flops=4_000_000_000, bytes_accessed=10_000_000, transcendentals=3_000_000
        ),
    )(q, k, v, cq, hk, hv, w, cot.T, frame_ids.reshape(16, 128), masked.reshape(16, 128))
    final = pl.pallas_call(
        finish,
        out_shape=kinds,
        in_specs=[away] * 8,
        out_specs=[away] * 8,
        scratch_shapes=[
            *[pltpu.VMEM(kind.shape, kind.dtype) for kind in kinds],
            pltpu.SemaphoreType.DMA((16,)),
        ],
        compiler_params=pltpu.CompilerParams(vmem_limit_bytes=60 * 2**20),
    )(*results)
    return (final[0].T, *final[1:7], final[7].T)


def solution(mesh):
    finer = Mesh(mesh.devices.reshape(2, NZ, NX, 2, 2), AXES)
    split = P(GRP, COLS)
    return jax.shard_map(
        on_device,
        mesh=finer,
        in_specs=(*[split] * 6, P(), P(), P(COLS, None), split),
        out_specs=(*[split] * 7, P(COLS, GRP)),
        check_vma=False,
    )
```

```python
import itertools

import jax
import jax.numpy as jnp
from jax import lax
from jax.experimental import pallas as pl
from jax.experimental.pallas import tpu as pltpu
from jax.sharding import Mesh
from jax.sharding import PartitionSpec as P

F32, BF16 = jnp.float32, jnp.bfloat16
HD = 128
FACTOR = HD**-0.5
NZ, NX = 8, 4
HIDDEN = -1e30
NEVER = 1e9
MESH = pl.DeviceIdType.MESH
AXES = ("yl", "z", "x", "core", "yh")
GRP, COLS = ("yl", "z"), ("x", "core", "yh")

K0, HK0, V0, HV0, KV_ROWS = 0, 256, 640, 896, 1280
OUT_AT = ((0, 128), (256, 128), (512, 128), (768, 128), (1024, 192), (1408, 192))
OUT_ROWS = 1792
TURN, TURN_OWN = 127, 47


def dot(a, b):
    return lax.dot_general(a, b, (((1,), (0,)), ((), ())), preferred_element_type=F32)


def dot_t(a, b):
    return lax.dot_general(a, b, (((1,), (1,)), ((), ())), preferred_element_type=F32)


def kernel(
    q, k, v, cq, hk, hv, w_hbm, cot, frames, masked,
    out_h, oq_h, ok_h, ov_h, ocq_h, ohk_h, ohv_h, wg_h,
    out, oq, ok, ov, ocq, ohk, ohv, wg, att_all, tall, kv, qs, gr, st, self_s, cross_s, m_s, l_s, acc_s, w, cf, part, core_in,
    mid, x_in, y_out, y_in, grad_out, att_out, ka, dqa, xo, row_q, row_k, row_p, col,
    send_sems, recv_sems, own_sems,
):
    yl, z, x = lax.axis_index("yl"), lax.axis_index("z"), lax.axis_index("x")
    core, yh = lax.axis_index("core"), lax.axis_index("yh")
    zp, zq = lax.rem(z, 2), lax.div(z, 2)
    upper, side = lax.div(z, 4), lax.rem(zq, 2)
    mate_y, mate_c, mate_h = {"yl": 1 - yl}, {"core": 1 - core}, {"yh": 1 - yh}
    mate_z, next_z = {"z": z + 1 - 2 * zp}, {"z": lax.rem(z + (NZ - 1) + 2 * zp, NZ)}
    blk = x * 2 + core
    tokens, chunk = yl * NZ + z, blk * 2 + yh

    def flip(fz, fy, fc):
        at = (1 - zp if fz else zp) * 4 + (1 - yl if fy else yl) * 2
        return at + (1 - core if fc else core)

    slot = flip(0, 0, 0)
    landing = zp * 4 + yl * 2 + upper
    swap_to = [{"z": zp + 4 * core + 2 * e, "core": upper} for e in range(2)]
    stays = [zq == 2 * core + e for e in range(2)]

    turned = {
        "yl": lax.div(chunk, NZ), "z": lax.rem(chunk, NZ), "x": lax.div(tokens, 4),
        "core": lax.rem(lax.div(tokens, 2), 2), "yh": lax.rem(tokens, 2),
    }

    def at_z(d):
        return lax.rem(z + (d + NZ), NZ)

    def at_x(d):
        return lax.rem(x + (d + NX), NX)

    flips = [(fz, fy, fc) for fz in (0, 1) for fy in (0, 1) for fc in (0, 1)][1:]
    group = [
        {"z": z + fz * (1 - 2 * zp), "yl": yl + fy * (1 - 2 * yl), "core": core + fc * (1 - 2 * core)}
        for fz, fy, fc in flips
    ]
    peers = [next_z, mate_h] + group + [{"x": at_x(d)} for d in range(1, NX)]
    barrier = pltpu.get_barrier_semaphore()
    for peer in peers:
        pl.semaphore_signal(barrier, inc=1, device_id=peer, device_id_type=MESH)
    expected = len(peers)
    for peer, here in zip(swap_to + [turned], stays + [tokens == chunk]):

        @pl.when(jnp.logical_not(here))
        def _():
            pl.semaphore_signal(barrier, inc=1, device_id=peer, device_id_type=MESH)

        expected = expected + 1 - here.astype(jnp.int32)

    def owner_z(i):
        return zp + 4 * core + 2 * i

    own_number = itertools.count()

    def bring(src, dst):
        copy = pltpu.make_async_copy(src, dst, own_sems.at[next(own_number)])
        copy.start()
        return copy

    def lanes(i):
        return pl.ds(pl.multiple_of(i * HD, HD), HD)

    def rows(base, i, n):
        return pl.ds(pl.multiple_of(base + i * n, 16), n)

    cot_own = bring(cot, cf.at[chunk])
    w_copy = bring(w_hbm, w)
    pl.semaphore_wait(barrier, expected)

    number = itertools.count()
    started, exchanged = [], []

    def send(src, dst, to):
        i = next(number)
        copy = pltpu.make_async_remote_copy(
            src_ref=src, dst_ref=dst, send_sem=send_sems.at[i], recv_sem=recv_sems.at[i],
            device_id=to, device_id_type=MESH,
        )
        copy.start()
        started.append(copy)
        return copy

    def exchange(arrays):
        messages = []
        for source, target in arrays:
            first, _ = next(number), next(number)
            for e in range(2):

                def remote(at, to_slot, to_side, to_owner, e=e, first=first, source=source, target=target):
                    return pltpu.make_async_remote_copy(
                        src_ref=source(e), dst_ref=target(to_slot, to_side, to_owner), send_sem=send_sems.at[first + e],
                        recv_sem=recv_sems.at[first + at], device_id=swap_to[e], device_id_type=MESH,
                    )

                local = pltpu.make_async_copy(source(e), target(slot, e, z), own_sems.at[next(own_number)])
                messages.append((e, remote(side, landing, side, owner_z(e)), remote(e, slot, e, z), local))
        for e in range(2):

            @pl.when(jnp.logical_not(stays[e]))
            def _():
                for to, out_copy, _, _ in messages:
                    if to == e:
                        out_copy.start()

            @pl.when(stays[e])
            def _():
                for to, _, _, local in messages:
                    if to == e:
                        local.start()

        exchanged.append(messages)
        return messages

    def wait_exchange(messages):
        for e in range(2):

            @pl.when(jnp.logical_not(stays[e]))
            def _():
                for to, _, in_copy, _ in messages:
                    if to == e:
                        in_copy.wait_recv()

            @pl.when(stays[e])
            def _():
                for to, _, _, local in messages:
                    if to == e:
                        local.wait()

    def to_slot(src, dst, base, n):
        return (
            lambda e: src.at[:, pl.ds(e * HD, HD)],
            lambda at, i, owner: dst.at[at, rows(base, i, n)],
        )

    k_moves = exchange([to_slot(k, kv, K0, 128), to_slot(hk, kv, HK0, 192)])
    v_moves = exchange([to_slot(v, kv, V0, 128), to_slot(hv, kv, HV0, 192)])
    cot_copy = send(cot, cf.at[chunk], mate_h)
    q_moves = exchange([to_slot(q, qs, 0, 128), to_slot(cq, qs, 256, 128)])
    t_copy = pltpu.make_async_remote_copy(
        src_ref=cot, dst_ref=tall.at[tokens], send_sem=send_sems.at[TURN], recv_sem=recv_sems.at[TURN],
        device_id=turned, device_id_type=MESH,
    )
    t_own = pltpu.make_async_copy(cot, tall.at[tokens], own_sems.at[TURN_OWN])

    @pl.when(tokens != chunk)
    def _():
        t_copy.start()

    @pl.when(tokens == chunk)
    def _():
        t_own.start()

    own_frames = frames[...].astype(F32)
    key_frames = jnp.where(masked[...] == 0, own_frames, NEVER)
    lane = lax.broadcasted_iota(jnp.int32, (1, 128), 1)
    for o in range(8):
        for i in range(2):
            t = (o // 2 % 2) * NZ + o // 4 + 4 * (o % 2) + 2 * i
            at = pl.ds(128 * i, 128)
            row_q[o : o + 1, at] = own_frames[t : t + 1]
            row_k[o : o + 1, at] = key_frames[t : t + 1]
            row_p[o : o + 1, at] = (lane + t * 128).astype(F32)
    which = lax.broadcasted_iota(jnp.int32, (HD, 256), 0)
    spread = jnp.where(which == 0, row_q[pl.ds(slot, 1), :], row_k[pl.ds(slot, 1), :])
    col[...] = jnp.where(which == 2, row_p[pl.ds(slot, 1), :], spread).T

    def part_of(ref, start, n):
        return lambda o: ref.at[o, pl.ds(start, n)]

    def spread_first(view):
        mine = view(slot)
        return [send(mine, mine, mate_z), send(mine, mine, mate_y), send(mine, mine, mate_c)]

    def spread_second(view, before):
        before[0].wait_recv()
        got = view(flip(1, 0, 0))
        made = [send(got, got, mate_y), send(got, got, mate_c)]
        before[1].wait_recv()
        got = view(flip(0, 1, 0))
        return [*made, send(got, got, mate_c)]

    def spread_third(view, before):
        before[0].wait_recv()
        got = view(flip(1, 1, 0))
        return send(got, got, mate_c)

    k_view, v_view = part_of(kv, 0, V0), part_of(kv, V0, V0)
    q_view, g_view = part_of(qs, 0, 512), part_of(gr, 0, 256)

    def ring_step(view, s, before):
        for copy in before:
            copy.wait_recv()
        right, left = {"z": at_z(1)}, {"z": at_z(-1)}
        last = s == NZ // 2 - 1
        from_r, from_l = view(at_z(-s), 0 if last else None), view(at_z(s), 1 if last else None)
        return [send(from_r, from_r, right), send(from_l, from_l, left)]

    def att_view(o, part):
        return att_all.at[yl, o] if part is None else att_all.at[yl, o, pl.ds(part * 64, 64)]

    def wait_all(copies):
        for copy in copies:
            copy.wait_recv()

    m_s[...] = jnp.full(m_s.shape, HIDDEN, F32)
    l_s[...] = jnp.zeros(l_s.shape, F32)
    acc_s[...] = jnp.zeros(acc_s.shape, F32)

    def take_in(i, s, values):
        top = m_s[i]
        new = jnp.maximum(top, jnp.max(s, axis=1, keepdims=True))
        p = jnp.exp(s - new)
        shrink = jnp.exp(top - new)
        l_s[i] = l_s[i] * shrink + jnp.sum(p, axis=1, keepdims=True)
        acc_s[i] = acc_s[i] * shrink + dot(p.astype(BF16), values)
        m_s[i] = new

    def attend(o):
        s = dot_t(qs[slot, 0:256, :], kv[o, K0 : K0 + 256, :]) * FACTOR
        keep = (row_k[pl.ds(o, 1), :] <= col[:, 0:1]) | (row_p[pl.ds(o, 1), :] == col[:, 2:3])
        s = jnp.where(keep, s, HIDDEN)
        self_s[o] = s
        take_in(0, s, kv[o, V0 : V0 + 256, :])
        s = dot_t(qs[slot, 256:512, :], kv[o, HK0 : HK0 + 384, :]) * FACTOR
        cross_s[o] = s
        take_in(1, s, kv[o, HV0 : HV0 + 384, :])

    def both_cores(work, fz, fy):
        def body(i, carry):
            work(flip(fz, fy, 0) - core + lax.rem(core + i, 2))
            return carry

        lax.fori_loop(0, 2, body, 0)

    def pair(ref, d):
        return ref.at[pl.ds((at_x(d) * 2 + core) * 2, 2)]

    def one(ref, d, i):
        return ref.at[(at_x(d) * 2 + core) * 2 + i]

    def x_first(ref):
        mine = pair(ref, 0)
        return [send(mine, mine, {"x": at_x(1)}), send(mine, mine, {"x": at_x(-1)}), send(mine, mine, mate_c)]

    def x_second(ref, before):
        before[0].wait_recv()
        far = one(ref, -1, 0)
        made = [send(far, far, {"x": at_x(1)})]
        cores = [before[2], send(pair(ref, -1), pair(ref, -1), mate_c)]
        before[1].wait_recv()
        far = one(ref, 1, 1)
        made.append(send(far, far, {"x": at_x(-1)}))
        cores.append(send(pair(ref, 1), pair(ref, 1), mate_c))
        return made, cores

    def x_third(ref, before):
        made, cores = before
        wait_all(made)
        return cores + [send(pair(ref, 2), pair(ref, 2), mate_c)]

    wait_exchange(k_moves)
    k1 = spread_first(k_view)
    wait_exchange(v_moves)
    v1 = spread_first(v_view)
    cot_own.wait()
    cot_copy.wait_recv()
    c_first = x_first(cf)
    wait_exchange(q_moves)
    q1 = spread_first(q_view)
    attend(slot)
    k2 = spread_second(k_view, k1)
    c_second = x_second(cf, c_first)
    v2 = spread_second(v_view, v1)
    wait_all([k1[2], v1[2]])
    attend(flip(0, 0, 1))
    c_core = x_third(cf, c_second)

    @pl.when(tokens != chunk)
    def _():
        t_copy.wait()

    @pl.when(tokens == chunk)
    def _():
        t_own.wait()

    turn_h = send(tall.at[chunk], tall.at[chunk], mate_h)

    wait_all(c_core)
    w_copy.wait()
    grad = dot(w[:, 0:640], cf[0:2].reshape(640, HD))
    for b in range(1, 8):
        grad = grad + dot(w[:, 640 * b : 640 * (b + 1)], cf[2 * b : 2 * b + 2].reshape(640, HD))
    grad_out[...] = grad.T.astype(BF16)
    g_moves = exchange([to_slot(grad_out, gr, 0, 128)])
    q2 = spread_second(q_view, q1)
    wait_all([k2[1], v2[1], k2[2], v2[2]])
    both_cores(attend, 1, 0)
    wait_exchange(g_moves)
    g1 = spread_first(g_view)
    turn_h.wait_recv()
    turn_first = x_first(tall)
    both_cores(attend, 0, 1)
    k3 = spread_third(k_view, k2)
    v3 = spread_third(v_view, v2)
    attend(flip(1, 1, 0))
    q3 = spread_third(q_view, q2)
    wait_all([k3, v3])
    attend(flip(1, 1, 1))

    heads = [acc_s[i] / l_s[i] for i in range(2)]
    logs = [m_s[i] + jnp.log(l_s[i]) for i in range(2)]
    att = (heads[0] + heads[1]).astype(BF16)
    att_out[...] = att
    a_moves = exchange(
        [(lambda e: att_out.at[pl.ds(e * 128, 128)], lambda at, i, owner: att_all.at[yl, owner, :, lanes(i)])]
    )

    def to_mate(o):
        return send(att_view(o, None), att_view(o, None), mate_y)

    g_own = gr[slot].astype(F32)
    dots = [jnp.sum(g_own * heads[i], axis=1, keepdims=True) for i in range(2)]
    lane = lax.broadcasted_iota(jnp.int32, (256, HD), 1)
    table = jnp.zeros((256, HD), F32)
    for i, column in enumerate(logs + dots):
        table = jnp.where(lane == i, column, table)
    st[slot] = table.T[0:8, :]
    s_copies = [send(st.at[slot], st.at[slot], peer) for peer in group]
    g2 = spread_second(g_view, g1)
    turn_second = x_second(tall, turn_first)
    wait_exchange(a_moves)

    t0 = ring_step(att_view, 0, [])
    turn_core = x_third(tall, turn_second)
    t_mate = [to_mate(z)]

    own_att = att_all[yl, z]
    for b in range(8):
        part[b] = dot(own_att, w[:, 640 * b : 640 * (b + 1)]).astype(BF16)
    p_core = [
        send(part.at[2 * i + (1 - core)], core_in.at[i], mate_c) for i in range(NX)
    ]

    def query_side(o, carry):
        g = gr[slot]
        p = jnp.exp(self_s[o] - logs[0])
        d = dot_t(g, kv[o, V0 : V0 + 256, :])
        ds = (p * (d - dots[0])).astype(BF16)
        dqa[0] += dot(ds, kv[o, K0 : K0 + 256, :])
        p = jnp.exp(cross_s[o] - logs[1])
        d = dot_t(g, kv[o, HV0 : HV0 + 384, :])
        ds = (p * (d - dots[1])).astype(BF16)
        dqa[1] += dot(ds, kv[o, HK0 : HK0 + 384, :])
        return carry

    dqa[...] = jnp.zeros(dqa.shape, F32)
    lax.fori_loop(0, 4, query_side, 0)

    wait_all(p_core)

    def add_cores(i, carry):
        both = part[2 * i + core].astype(F32) + core_in[i].astype(F32)
        mid[i] = both.astype(BF16)
        return carry

    lax.fori_loop(0, NX, add_cores, 0)
    p_x = [send(mid.at[at_x(d)], x_in.at[d - 1], {"x": at_x(d)}) for d in (1, 3, 2)]
    g3 = spread_third(g_view, g2)
    t1 = ring_step(att_view, 1, t0)
    t_mate += [to_mate(at_z(1)), to_mate(at_z(-1))]

    lax.fori_loop(4, 8, query_side, 0)
    t2 = ring_step(att_view, 2, t1)
    t_mate += [to_mate(at_z(2)), to_mate(at_z(-2))]

    def give_back(i, ref, values):
        base, n = OUT_AT[i]
        xo[base : base + 2 * n, :] = values.astype(BF16)
        return (lambda e: xo.at[pl.ds(base + e * n, n)], lambda at, j, owner: ref.at[:, lanes(j)])

    dq_moves = exchange([give_back(0, oq, dqa[0] * FACTOR), give_back(1, ocq, dqa[1] * FACTOR)])

    wait_all(s_copies)
    ka[...] = jnp.zeros(ka.shape, F32)

    def key_side(o):
        g = gr[o]
        keep = (col[:, 1:2] <= row_q[pl.ds(o, 1), :]) | (col[:, 2:3] == row_p[pl.ds(o, 1), :])
        s = jnp.where(keep, dot_t(kv[slot, K0 : K0 + 256, :], qs[o, 0:256, :]) * FACTOR, HIDDEN)
        for qq, stat, at_k, at_v, n in ((qs[o, 0:256, :], 0, K0, V0, 256), (qs[o, 256:512, :], 1, HK0, HV0, 384)):
            if stat == 1:
                s = dot_t(kv[slot, at_k : at_k + n, :], qq) * FACTOR
            p = jnp.exp(s - st[o, stat : stat + 1, :])
            ka[at_v : at_v + n, :] += dot(p.astype(BF16), g)
            d = dot_t(kv[slot, at_v : at_v + n, :], g)
            ds = (p * (d - st[o, stat + 2 : stat + 3, :])).astype(BF16)
            ka[at_k : at_k + n, :] += dot(ds, qq)

    key_side(slot)
    wait_all([q1[2], g1[2]])
    key_side(flip(0, 0, 1))
    wait_all([q2[1], g2[1]])
    both_cores(key_side, 1, 0)

    wait_all(p_x)
    total = mid[x].astype(F32)
    for d in range(3):
        total = total + x_in[d].astype(F32)
    y_out[...] = total.T
    y_in[0] = y_out[pl.ds(pl.multiple_of((1 - yh) * 320, 64), 320), :].astype(BF16)
    p_y = send(y_in.at[0], y_in.at[1], mate_h)

    t3 = ring_step(att_view, 3, t2)
    t_mate += [to_mate(at_z(3)), to_mate(at_z(-3))]
    wait_all([q2[2], g2[2]])
    both_cores(key_side, 0, 1)
    wait_all([q3, g3])
    both_cores(key_side, 1, 1)
    dk_moves = exchange(
        [
            give_back(2, ok, ka[K0 : K0 + 256, :] * FACTOR),
            give_back(3, ov, ka[V0 : V0 + 256, :]),
            give_back(4, ohk, ka[HK0 : HK0 + 384, :] * FACTOR),
            give_back(5, ohv, ka[HV0 : HV0 + 384, :]),
        ]
    )
    wait_all(t3)
    t_mate.append(to_mate(at_z(4)))

    p_y.wait_recv()
    own_total = y_out[pl.ds(pl.multiple_of(yh * 320, 64), 320), :]
    out[...] = (own_total + y_in[1].astype(F32)).astype(BF16)
    leaving = [bring(out, out_h)]
    wait_exchange(dq_moves)
    leaving += [bring(oq, oq_h), bring(ocq, ocq_h)]
    wait_all(turn_core)
    wait_all(t_mate)
    total = jnp.zeros((320, 256), F32)
    for half in range(2):
        for o in range(NZ):
            total = total + dot(tall[half * NZ + o], att_all[half, o])
    wg[...] = total
    leaving.append(bring(wg, wg_h))
    wait_exchange(dk_moves)
    leaving += [bring(a, b) for a, b in ((ok, ok_h), (ov, ov_h), (ohk, ohk_h), (ohv, ohv_h))]
    for copy in started:
        copy.wait_send()
    for e in range(2):

        @pl.when(jnp.logical_not(stays[e]))
        def _():
            for messages in exchanged:
                for to, out_copy, _, _ in messages:
                    if to == e:
                        out_copy.wait_send()

    for copy in leaving:
        copy.wait()


def finish(*refs):
    sources, outs, held, sems = refs[0:8], refs[8:16], refs[16:24], refs[24]
    inward = [pltpu.make_async_copy(s, h, sems.at[i]) for i, (s, h) in enumerate(zip(sources, held))]
    outward = [pltpu.make_async_copy(h, o, sems.at[8 + i]) for i, (h, o) in enumerate(zip(held, outs))]
    for copy in inward:
        copy.start()
    for copy, onward in zip(inward, outward):
        copy.wait()
        onward.start()
    for copy in outward:
        copy.wait()


def on_device(q, k, v, cq, hk, hv, frame_ids, masked, w, cot):
    vmem = pl.BlockSpec(memory_space=pltpu.VMEM)
    shape = jax.ShapeDtypeStruct
    away = pl.BlockSpec(memory_space=pl.ANY)
    kinds = (shape((320, 128), BF16), *[shape((128, 256), BF16)] * 4, *[shape((192, 256), BF16)] * 2, shape((320, 256), F32))
    results = pl.pallas_call(
        kernel,
        out_shape=kinds,
        in_specs=[away] * 8 + [vmem] * 2,
        out_specs=[away] * 8,
        scratch_shapes=[
            *[pltpu.VMEM(kind.shape, kind.dtype) for kind in kinds],
            pltpu.VMEM((2, NZ, 128, 256), BF16),
            pltpu.VMEM((2 * NZ, 320, HD), BF16),
            pltpu.VMEM((NZ, KV_ROWS, HD), BF16),
            pltpu.VMEM((NZ, 512, HD), BF16),
            pltpu.VMEM((NZ, 256, HD), BF16),
            pltpu.VMEM((NZ, 8, 256), F32),
            pltpu.VMEM((NZ, 256, 256), F32),
            pltpu.VMEM((NZ, 256, 384), F32),
            pltpu.VMEM((2, 256, 1), F32),
            pltpu.VMEM((2, 256, 1), F32),
            pltpu.VMEM((2, 256, HD), F32),
            pltpu.VMEM((256, 5120), BF16),
            pltpu.VMEM((16, 320, HD), BF16),
            pltpu.VMEM((8, 128, 640), BF16),
            pltpu.VMEM((NX, 128, 640), BF16),
            pltpu.VMEM((NX, 128, 640), BF16),
            pltpu.VMEM((NX - 1, 128, 640), BF16),
            pltpu.VMEM((640, HD), F32),
            pltpu.VMEM((2, 320, HD), BF16),
            pltpu.VMEM((128, 256), BF16),
            pltpu.VMEM((256, HD), BF16),
            pltpu.VMEM((KV_ROWS, HD), F32),
            pltpu.VMEM((2, 256, HD), F32),
            pltpu.VMEM((OUT_ROWS, HD), BF16),
            *[pltpu.VMEM((NZ, 256), F32)] * 3,
            pltpu.VMEM((256, HD), F32),
            pltpu.SemaphoreType.DMA((TURN + 1,)),
            pltpu.SemaphoreType.DMA((TURN + 1,)),
            pltpu.SemaphoreType.DMA((TURN_OWN + 1,)),
        ],
        compiler_params=pltpu.CompilerParams(
            collective_id=0, has_side_effects=True, vmem_limit_bytes=60 * 2**20
        ),
        cost_estimate=pl.CostEstimate(
            flops=4_000_000_000, bytes_accessed=10_000_000, transcendentals=3_000_000
        ),
    )(q, k, v, cq, hk, hv, w, cot.T, frame_ids.reshape(16, 128), masked.reshape(16, 128))
    final = pl.pallas_call(
        finish,
        out_shape=kinds,
        in_specs=[away] * 8,
        out_specs=[away] * 8,
        scratch_shapes=[
            *[pltpu.VMEM(kind.shape, kind.dtype) for kind in kinds],
            pltpu.SemaphoreType.DMA((16,)),
        ],
        compiler_params=pltpu.CompilerParams(vmem_limit_bytes=60 * 2**20),
    )(*results)
    return (final[0].T, *final[1:7], final[7].T)


def solution(mesh):
    finer = Mesh(mesh.devices.reshape(2, NZ, NX, 2, 2), AXES)
    split = P(GRP, COLS)
    return jax.shard_map(
        on_device,
        mesh=finer,
        in_specs=(*[split] * 6, P(), P(), P(COLS, None), split),
        out_specs=(*[split] * 7, P(COLS, GRP)),
        check_vma=False,
    )
```

```python
import itertools

import jax
import jax.numpy as jnp
from jax import lax
from jax.experimental import pallas as pl
from jax.experimental.pallas import tpu as pltpu
from jax.sharding import Mesh
from jax.sharding import PartitionSpec as P

F32, BF16 = jnp.float32, jnp.bfloat16
HD = 128
FACTOR = HD**-0.5
NZ, NX = 8, 4
HIDDEN = -1e30
NEVER = 1e9
MESH = pl.DeviceIdType.MESH
AXES = ("yl", "z", "x", "core", "yh")
GRP, COLS = ("yl", "z"), ("x", "core", "yh")

K0, HK0, V0, HV0, KV_ROWS = 0, 256, 640, 896, 1280
OUT_AT = ((0, 128), (256, 128), (512, 128), (768, 128), (1024, 192), (1408, 192))
OUT_ROWS = 1792
TURN, TURN_OWN = 127, 47


def dot(a, b):
    return lax.dot_general(a, b, (((1,), (0,)), ((), ())), preferred_element_type=F32)


def dot_t(a, b):
    return lax.dot_general(a, b, (((1,), (1,)), ((), ())), preferred_element_type=F32)


def kernel(
    q, k, v, cq, hk, hv, w_hbm, cot, frames, masked,
    out_h, oq_h, ok_h, ov_h, ocq_h, ohk_h, ohv_h, wg_h,
    out, oq, ok, ov, ocq, ohk, ohv, wg, att_all, tall, kv, qs, gr, st, self_s, cross_s, m_s, l_s, acc_s, w, cf, part, core_in,
    mid, x_in, y_out, y_in, grad_out, att_out, ka, dqa, xo, row_q, row_k, row_p, col,
    send_sems, recv_sems, own_sems,
):
    yl, z, x = lax.axis_index("yl"), lax.axis_index("z"), lax.axis_index("x")
    core, yh = lax.axis_index("core"), lax.axis_index("yh")
    zp, zq = lax.rem(z, 2), lax.div(z, 2)
    upper, side = lax.div(z, 4), lax.rem(zq, 2)
    mate_y, mate_c, mate_h = {"yl": 1 - yl}, {"core": 1 - core}, {"yh": 1 - yh}
    mate_z, next_z = {"z": z + 1 - 2 * zp}, {"z": lax.rem(z + (NZ - 1) + 2 * zp, NZ)}
    blk = x * 2 + core
    tokens, chunk = yl * NZ + z, blk * 2 + yh

    def flip(fz, fy, fc):
        at = (1 - zp if fz else zp) * 4 + (1 - yl if fy else yl) * 2
        return at + (1 - core if fc else core)

    slot = flip(0, 0, 0)
    landing = zp * 4 + yl * 2 + upper
    swap_to = [{"z": zp + 4 * core + 2 * e, "core": upper} for e in range(2)]
    stays = [zq == 2 * core + e for e in range(2)]

    turned = {
        "yl": lax.div(chunk, NZ), "z": lax.rem(chunk, NZ), "x": lax.div(tokens, 4),
        "core": lax.rem(lax.div(tokens, 2), 2), "yh": lax.rem(tokens, 2),
    }

    def at_z(d):
        return lax.rem(z + (d + NZ), NZ)

    def at_x(d):
        return lax.rem(x + (d + NX), NX)

    flips = [(fz, fy, fc) for fz in (0, 1) for fy in (0, 1) for fc in (0, 1)][1:]
    group = [
        {"z": z + fz * (1 - 2 * zp), "yl": yl + fy * (1 - 2 * yl), "core": core + fc * (1 - 2 * core)}
        for fz, fy, fc in flips
    ]
    peers = [next_z, mate_h] + group + [{"x": at_x(d)} for d in range(1, NX)]
    barrier = pltpu.get_barrier_semaphore()
    for peer in peers:
        pl.semaphore_signal(barrier, inc=1, device_id=peer, device_id_type=MESH)
    expected = len(peers)
    for peer, here in zip(swap_to + [turned], stays + [tokens == chunk]):

        @pl.when(jnp.logical_not(here))
        def _():
            pl.semaphore_signal(barrier, inc=1, device_id=peer, device_id_type=MESH)

        expected = expected + 1 - here.astype(jnp.int32)

    def owner_z(i):
        return zp + 4 * core + 2 * i

    own_number = itertools.count()

    def bring(src, dst):
        copy = pltpu.make_async_copy(src, dst, own_sems.at[next(own_number)])
        copy.start()
        return copy

    def lanes(i):
        return pl.ds(pl.multiple_of(i * HD, HD), HD)

    def rows(base, i, n):
        return pl.ds(pl.multiple_of(base + i * n, 16), n)

    cot_own = bring(cot, cf.at[chunk])
    w_copy = bring(w_hbm, w)
    pl.semaphore_wait(barrier, expected)

    number = itertools.count()
    started, exchanged = [], []

    def send(src, dst, to):
        i = next(number)
        copy = pltpu.make_async_remote_copy(
            src_ref=src, dst_ref=dst, send_sem=send_sems.at[i], recv_sem=recv_sems.at[i],
            device_id=to, device_id_type=MESH,
        )
        copy.start()
        started.append(copy)
        return copy

    def exchange(arrays):
        messages = []
        for source, target in arrays:
            first, _ = next(number), next(number)
            for e in range(2):

                def remote(at, to_slot, to_side, to_owner, e=e, first=first, source=source, target=target):
                    return pltpu.make_async_remote_copy(
                        src_ref=source(e), dst_ref=target(to_slot, to_side, to_owner), send_sem=send_sems.at[first + e],
                        recv_sem=recv_sems.at[first + at], device_id=swap_to[e], device_id_type=MESH,
                    )

                local = pltpu.make_async_copy(source(e), target(slot, e, z), own_sems.at[next(own_number)])
                messages.append((e, remote(side, landing, side, owner_z(e)), remote(e, slot, e, z), local))
        for e in range(2):

            @pl.when(jnp.logical_not(stays[e]))
            def _():
                for to, out_copy, _, _ in messages:
                    if to == e:
                        out_copy.start()

            @pl.when(stays[e])
            def _():
                for to, _, _, local in messages:
                    if to == e:
                        local.start()

        exchanged.append(messages)
        return messages

    def wait_exchange(messages):
        for e in range(2):

            @pl.when(jnp.logical_not(stays[e]))
            def _():
                for to, _, in_copy, _ in messages:
                    if to == e:
                        in_copy.wait_recv()

            @pl.when(stays[e])
            def _():
                for to, _, _, local in messages:
                    if to == e:
                        local.wait()

    def to_slot(src, dst, base, n):
        return (
            lambda e: src.at[:, pl.ds(e * HD, HD)],
            lambda at, i, owner: dst.at[at, rows(base, i, n)],
        )

    def wide(ref, t):
        return ref.at[lax.div(t, 2), :, lanes(lax.rem(t, 2))]

    k_moves = exchange([to_slot(k, kv, K0, 128), to_slot(hk, kv, HK0, 192)])
    v_moves = exchange([to_slot(v, kv, V0, 128), to_slot(hv, kv, HV0, 192)])
    cot_copy = send(cot, cf.at[chunk], mate_h)
    q_moves = exchange([to_slot(q, qs, 0, 128), to_slot(cq, qs, 256, 128)])
    t_copy = pltpu.make_async_remote_copy(
        src_ref=cot, dst_ref=wide(tall, tokens), send_sem=send_sems.at[TURN], recv_sem=recv_sems.at[TURN],
        device_id=turned, device_id_type=MESH,
    )
    t_own = pltpu.make_async_copy(cot, wide(tall, tokens), own_sems.at[TURN_OWN])

    @pl.when(tokens != chunk)
    def _():
        t_copy.start()

    @pl.when(tokens == chunk)
    def _():
        t_own.start()

    own_frames = frames[...].astype(F32)
    key_frames = jnp.where(masked[...] == 0, own_frames, NEVER)
    lane = lax.broadcasted_iota(jnp.int32, (1, 128), 1)
    for o in range(8):
        for i in range(2):
            t = (o // 2 % 2) * NZ + o // 4 + 4 * (o % 2) + 2 * i
            at = pl.ds(128 * i, 128)
            row_q[o : o + 1, at] = own_frames[t : t + 1]
            row_k[o : o + 1, at] = key_frames[t : t + 1]
            row_p[o : o + 1, at] = (lane + t * 128).astype(F32)
    which = lax.broadcasted_iota(jnp.int32, (HD, 256), 0)
    spread = jnp.where(which == 0, row_q[pl.ds(slot, 1), :], row_k[pl.ds(slot, 1), :])
    col[...] = jnp.where(which == 2, row_p[pl.ds(slot, 1), :], spread).T

    def part_of(ref, start, n):
        return lambda o: ref.at[o, pl.ds(start, n)]

    def spread_first(view):
        mine = view(slot)
        return [send(mine, mine, mate_z), send(mine, mine, mate_y), send(mine, mine, mate_c)]

    def spread_second(view, before):
        before[0].wait_recv()
        got = view(flip(1, 0, 0))
        made = [send(got, got, mate_y), send(got, got, mate_c)]
        before[1].wait_recv()
        got = view(flip(0, 1, 0))
        return [*made, send(got, got, mate_c)]

    def spread_third(view, before):
        before[0].wait_recv()
        got = view(flip(1, 1, 0))
        return send(got, got, mate_c)

    k_view, v_view = part_of(kv, 0, V0), part_of(kv, V0, V0)
    q_view, g_view = part_of(qs, 0, 512), part_of(gr, 0, 256)

    def ring_step(view, s, before):
        for copy in before:
            copy.wait_recv()
        right, left = {"z": at_z(1)}, {"z": at_z(-1)}
        last = s == NZ // 2 - 1
        from_r, from_l = view(at_z(-s), 0 if last else None), view(at_z(s), 1 if last else None)
        return [send(from_r, from_r, right), send(from_l, from_l, left)]

    def att_view(o, part):
        return att_all.at[yl, o] if part is None else att_all.at[yl, o, pl.ds(part * 64, 64)]

    def wait_all(copies):
        for copy in copies:
            copy.wait_recv()

    m_s[...] = jnp.full(m_s.shape, HIDDEN, F32)
    l_s[...] = jnp.zeros(l_s.shape, F32)
    acc_s[...] = jnp.zeros(acc_s.shape, F32)

    def take_in(i, s, values):
        top = m_s[i]
        new = jnp.maximum(top, jnp.max(s, axis=1, keepdims=True))
        p = jnp.exp(s - new)
        shrink = jnp.exp(top - new)
        l_s[i] = l_s[i] * shrink + jnp.sum(p, axis=1, keepdims=True)
        acc_s[i] = acc_s[i] * shrink + dot(p.astype(BF16), values)
        m_s[i] = new

    def attend(o):
        s = dot_t(qs[slot, 0:256, :], kv[o, K0 : K0 + 256, :]) * FACTOR
        keep = (row_k[pl.ds(o, 1), :] <= col[:, 0:1]) | (row_p[pl.ds(o, 1), :] == col[:, 2:3])
        s = jnp.where(keep, s, HIDDEN)
        self_s[o] = s
        take_in(0, s, kv[o, V0 : V0 + 256, :])
        s = dot_t(qs[slot, 256:512, :], kv[o, HK0 : HK0 + 384, :]) * FACTOR
        cross_s[o] = s
        take_in(1, s, kv[o, HV0 : HV0 + 384, :])

    def both_cores(work, fz, fy):
        def body(i, carry):
            work(flip(fz, fy, 0) - core + lax.rem(core + i, 2))
            return carry

        lax.fori_loop(0, 2, body, 0)

    def pair(ref, d):
        b = at_x(d) * 2 + core
        return ref.at[b] if ref is tall else ref.at[pl.ds(b * 2, 2)]

    def one(ref, d, i):
        b = (at_x(d) * 2 + core) * 2 + i
        return wide(ref, b) if ref is tall else ref.at[b]

    def x_first(ref):
        mine = pair(ref, 0)
        return [send(mine, mine, {"x": at_x(1)}), send(mine, mine, {"x": at_x(-1)}), send(mine, mine, mate_c)]

    def x_second(ref, before):
        before[0].wait_recv()
        far = one(ref, -1, 0)
        made = [send(far, far, {"x": at_x(1)})]
        cores = [before[2], send(pair(ref, -1), pair(ref, -1), mate_c)]
        before[1].wait_recv()
        far = one(ref, 1, 1)
        made.append(send(far, far, {"x": at_x(-1)}))
        cores.append(send(pair(ref, 1), pair(ref, 1), mate_c))
        return made, cores

    def x_third(ref, before):
        made, cores = before
        wait_all(made)
        return cores + [send(pair(ref, 2), pair(ref, 2), mate_c)]

    wait_exchange(k_moves)
    k1 = spread_first(k_view)
    wait_exchange(v_moves)
    v1 = spread_first(v_view)
    cot_own.wait()
    cot_copy.wait_recv()
    c_first = x_first(cf)
    wait_exchange(q_moves)
    q1 = spread_first(q_view)
    attend(slot)
    k2 = spread_second(k_view, k1)
    c_second = x_second(cf, c_first)
    v2 = spread_second(v_view, v1)
    wait_all([k1[2], v1[2]])
    attend(flip(0, 0, 1))
    c_core = x_third(cf, c_second)

    @pl.when(tokens != chunk)
    def _():
        t_copy.wait()

    @pl.when(tokens == chunk)
    def _():
        t_own.wait()

    turn_h = send(wide(tall, chunk), wide(tall, chunk), mate_h)

    wait_all(c_core)
    w_copy.wait()
    grad = dot(w[:, 0:640], cf[0:2].reshape(640, HD))
    for b in range(1, 8):
        grad = grad + dot(w[:, 640 * b : 640 * (b + 1)], cf[2 * b : 2 * b + 2].reshape(640, HD))
    grad_out[...] = grad.T.astype(BF16)
    g_moves = exchange([to_slot(grad_out, gr, 0, 128)])
    q2 = spread_second(q_view, q1)
    wait_all([k2[1], v2[1], k2[2], v2[2]])
    both_cores(attend, 1, 0)
    wait_exchange(g_moves)
    g1 = spread_first(g_view)
    turn_h.wait_recv()
    turn_first = x_first(tall)
    both_cores(attend, 0, 1)
    k3 = spread_third(k_view, k2)
    v3 = spread_third(v_view, v2)
    attend(flip(1, 1, 0))
    q3 = spread_third(q_view, q2)
    wait_all([k3, v3])
    attend(flip(1, 1, 1))

    heads = [acc_s[i] / l_s[i] for i in range(2)]
    logs = [m_s[i] + jnp.log(l_s[i]) for i in range(2)]
    att = (heads[0] + heads[1]).astype(BF16)
    att_out[...] = att
    a_moves = exchange(
        [(lambda e: att_out.at[pl.ds(e * 128, 128)], lambda at, i, owner: att_all.at[yl, owner, :, lanes(i)])]
    )

    def to_mate(o):
        return send(att_view(o, None), att_view(o, None), mate_y)

    g_own = gr[slot].astype(F32)
    dots = [jnp.sum(g_own * heads[i], axis=1, keepdims=True) for i in range(2)]
    lane = lax.broadcasted_iota(jnp.int32, (256, HD), 1)
    table = jnp.zeros((256, HD), F32)
    for i, column in enumerate(logs + dots):
        table = jnp.where(lane == i, column, table)
    st[slot] = table.T[0:8, :]
    s_copies = [send(st.at[slot], st.at[slot], peer) for peer in group]
    g2 = spread_second(g_view, g1)
    turn_second = x_second(tall, turn_first)
    wait_exchange(a_moves)

    t0 = ring_step(att_view, 0, [])
    turn_core = x_third(tall, turn_second)
    t_mate = [to_mate(z)]

    own_att = att_all[yl, z]
    for b in range(8):
        part[b] = dot(own_att, w[:, 640 * b : 640 * (b + 1)]).astype(BF16)
    p_core = [
        send(part.at[2 * i + (1 - core)], core_in.at[i], mate_c) for i in range(NX)
    ]

    def query_side(o, carry):
        g = gr[slot]
        p = jnp.exp(self_s[o] - logs[0])
        d = dot_t(g, kv[o, V0 : V0 + 256, :])
        ds = (p * (d - dots[0])).astype(BF16)
        dqa[0] += dot(ds, kv[o, K0 : K0 + 256, :])
        p = jnp.exp(cross_s[o] - logs[1])
        d = dot_t(g, kv[o, HV0 : HV0 + 384, :])
        ds = (p * (d - dots[1])).astype(BF16)
        dqa[1] += dot(ds, kv[o, HK0 : HK0 + 384, :])
        return carry

    dqa[...] = jnp.zeros(dqa.shape, F32)
    lax.fori_loop(0, 4, query_side, 0)

    wait_all(p_core)

    def add_cores(i, carry):
        both = part[2 * i + core].astype(F32) + core_in[i].astype(F32)
        mid[i] = both.astype(BF16)
        return carry

    lax.fori_loop(0, NX, add_cores, 0)
    p_x = [send(mid.at[at_x(d)], x_in.at[d - 1], {"x": at_x(d)}) for d in (1, 3, 2)]
    g3 = spread_third(g_view, g2)
    t1 = ring_step(att_view, 1, t0)
    t_mate += [to_mate(at_z(1)), to_mate(at_z(-1))]

    lax.fori_loop(4, 8, query_side, 0)
    t2 = ring_step(att_view, 2, t1)
    t_mate += [to_mate(at_z(2)), to_mate(at_z(-2))]

    def give_back(i, ref, values):
        base, n = OUT_AT[i]
        xo[base : base + 2 * n, :] = values.astype(BF16)
        return (lambda e: xo.at[pl.ds(base + e * n, n)], lambda at, j, owner: ref.at[:, lanes(j)])

    dq_moves = exchange([give_back(0, oq, dqa[0] * FACTOR), give_back(1, ocq, dqa[1] * FACTOR)])

    wait_all(s_copies)
    ka[...] = jnp.zeros(ka.shape, F32)

    def key_side(o):
        g = gr[o]
        keep = (col[:, 1:2] <= row_q[pl.ds(o, 1), :]) | (col[:, 2:3] == row_p[pl.ds(o, 1), :])
        s = jnp.where(keep, dot_t(kv[slot, K0 : K0 + 256, :], qs[o, 0:256, :]) * FACTOR, HIDDEN)
        for qq, stat, at_k, at_v, n in ((qs[o, 0:256, :], 0, K0, V0, 256), (qs[o, 256:512, :], 1, HK0, HV0, 384)):
            if stat == 1:
                s = dot_t(kv[slot, at_k : at_k + n, :], qq) * FACTOR
            p = jnp.exp(s - st[o, stat : stat + 1, :])
            ka[at_v : at_v + n, :] += dot(p.astype(BF16), g)
            d = dot_t(kv[slot, at_v : at_v + n, :], g)
            ds = (p * (d - st[o, stat + 2 : stat + 3, :])).astype(BF16)
            ka[at_k : at_k + n, :] += dot(ds, qq)

    key_side(slot)
    wait_all([q1[2], g1[2]])
    key_side(flip(0, 0, 1))
    wait_all([q2[1], g2[1]])
    both_cores(key_side, 1, 0)

    wait_all(p_x)
    total = mid[x].astype(F32)
    for d in range(3):
        total = total + x_in[d].astype(F32)
    y_out[...] = total.T
    y_in[0] = y_out[pl.ds(pl.multiple_of((1 - yh) * 320, 64), 320), :].astype(BF16)
    p_y = send(y_in.at[0], y_in.at[1], mate_h)

    t3 = ring_step(att_view, 3, t2)
    t_mate += [to_mate(at_z(3)), to_mate(at_z(-3))]
    wait_all([q2[2], g2[2]])
    both_cores(key_side, 0, 1)
    wait_all([q3, g3])
    both_cores(key_side, 1, 1)
    dk_moves = exchange(
        [
            give_back(2, ok, ka[K0 : K0 + 256, :] * FACTOR),
            give_back(3, ov, ka[V0 : V0 + 256, :]),
            give_back(4, ohk, ka[HK0 : HK0 + 384, :] * FACTOR),
            give_back(5, ohv, ka[HV0 : HV0 + 384, :]),
        ]
    )
    wait_all(t3)
    t_mate.append(to_mate(at_z(4)))

    p_y.wait_recv()
    own_total = y_out[pl.ds(pl.multiple_of(yh * 320, 64), 320), :]
    out[...] = (own_total + y_in[1].astype(F32)).astype(BF16)
    leaving = [bring(out, out_h)]
    wait_exchange(dq_moves)
    leaving += [bring(oq, oq_h), bring(ocq, ocq_h)]
    wait_all(turn_core)
    wait_all(t_mate)
    total = jnp.zeros((320, 256), F32)
    for i in range(NZ):
        half, o = i // 4, i % 4 * 2
        total = total + dot(tall[i], att_all[half, o : o + 2].reshape(256, 256))
    wg[...] = total
    leaving.append(bring(wg, wg_h))
    wait_exchange(dk_moves)
    leaving += [bring(a, b) for a, b in ((ok, ok_h), (ov, ov_h), (ohk, ohk_h), (ohv, ohv_h))]
    for copy in started:
        copy.wait_send()
    for e in range(2):

        @pl.when(jnp.logical_not(stays[e]))
        def _():
            for messages in exchanged:
                for to, out_copy, _, _ in messages:
                    if to == e:
                        out_copy.wait_send()

    for copy in leaving:
        copy.wait()


def finish(*refs):
    sources, outs, held, sems = refs[0:8], refs[8:16], refs[16:24], refs[24]
    inward = [pltpu.make_async_copy(s, h, sems.at[i]) for i, (s, h) in enumerate(zip(sources, held))]
    outward = [pltpu.make_async_copy(h, o, sems.at[8 + i]) for i, (h, o) in enumerate(zip(held, outs))]
    for copy in inward:
        copy.start()
    for copy, onward in zip(inward, outward):
        copy.wait()
        onward.start()
    for copy in outward:
        copy.wait()


def on_device(q, k, v, cq, hk, hv, frame_ids, masked, w, cot):
    vmem = pl.BlockSpec(memory_space=pltpu.VMEM)
    shape = jax.ShapeDtypeStruct
    away = pl.BlockSpec(memory_space=pl.ANY)
    kinds = (shape((320, 128), BF16), *[shape((128, 256), BF16)] * 4, *[shape((192, 256), BF16)] * 2, shape((320, 256), F32))
    results = pl.pallas_call(
        kernel,
        out_shape=kinds,
        in_specs=[away] * 8 + [vmem] * 2,
        out_specs=[away] * 8,
        scratch_shapes=[
            *[pltpu.VMEM(kind.shape, kind.dtype) for kind in kinds],
            pltpu.VMEM((2, NZ, 128, 256), BF16),
            pltpu.VMEM((NZ, 320, 256), BF16),
            pltpu.VMEM((NZ, KV_ROWS, HD), BF16),
            pltpu.VMEM((NZ, 512, HD), BF16),
            pltpu.VMEM((NZ, 256, HD), BF16),
            pltpu.VMEM((NZ, 8, 256), F32),
            pltpu.VMEM((NZ, 256, 256), F32),
            pltpu.VMEM((NZ, 256, 384), F32),
            pltpu.VMEM((2, 256, 1), F32),
            pltpu.VMEM((2, 256, 1), F32),
            pltpu.VMEM((2, 256, HD), F32),
            pltpu.VMEM((256, 5120), BF16),
            pltpu.VMEM((16, 320, HD), BF16),
            pltpu.VMEM((8, 128, 640), BF16),
            pltpu.VMEM((NX, 128, 640), BF16),
            pltpu.VMEM((NX, 128, 640), BF16),
            pltpu.VMEM((NX - 1, 128, 640), BF16),
            pltpu.VMEM((640, HD), F32),
            pltpu.VMEM((2, 320, HD), BF16),
            pltpu.VMEM((128, 256), BF16),
            pltpu.VMEM((256, HD), BF16),
            pltpu.VMEM((KV_ROWS, HD), F32),
            pltpu.VMEM((2, 256, HD), F32),
            pltpu.VMEM((OUT_ROWS, HD), BF16),
            *[pltpu.VMEM((NZ, 256), F32)] * 3,
            pltpu.VMEM((256, HD), F32),
            pltpu.SemaphoreType.DMA((TURN + 1,)),
            pltpu.SemaphoreType.DMA((TURN + 1,)),
            pltpu.SemaphoreType.DMA((TURN_OWN + 1,)),
        ],
        compiler_params=pltpu.CompilerParams(
            collective_id=0, has_side_effects=True, vmem_limit_bytes=60 * 2**20
        ),
        cost_estimate=pl.CostEstimate(
            flops=4_000_000_000, bytes_accessed=10_000_000, transcendentals=3_000_000
        ),
    )(q, k, v, cq, hk, hv, w, cot.T, frame_ids.reshape(16, 128), masked.reshape(16, 128))
    final = pl.pallas_call(
        finish,
        out_shape=kinds,
        in_specs=[away] * 8,
        out_specs=[away] * 8,
        scratch_shapes=[
            *[pltpu.VMEM(kind.shape, kind.dtype) for kind in kinds],
            pltpu.SemaphoreType.DMA((16,)),
        ],
        compiler_params=pltpu.CompilerParams(vmem_limit_bytes=60 * 2**20),
    )(*results)
    return (final[0].T, *final[1:7], final[7].T)


def solution(mesh):
    finer = Mesh(mesh.devices.reshape(2, NZ, NX, 2, 2), AXES)
    split = P(GRP, COLS)
    return jax.shard_map(
        on_device,
        mesh=finer,
        in_specs=(*[split] * 6, P(), P(), P(COLS, None), split),
        out_specs=(*[split] * 7, P(COLS, GRP)),
        check_vma=False,
    )
```
